256 devices in a mesh: shot: 16 (over x_hi, z), lag: 16 (over x_lo, y, core).
Axes of the slice: x: 4 (x_hi: 2, x_lo: 2; x = x_hi * 2 + x_lo), y: 4, z: 8, core: 2. Of those that a mesh axis runs over, the one named last changes fastest.
Arguments:
- traces: bfloat16 [96, 256, 8192], P('shot', 'lag'), may hold values from -64 to 64, as said below
- live_mask: int32 [96, 256], P('shot', 'lag'), may hold values 0 or 1
- gap_samples: int32 [1], replicated, may hold values from 1 to 32
Outputs:
- residual_traces: bfloat16 [96, 256, 8192], P('shot', 'lag')
The draws below stay inside these ranges and needn't reach their ends.
Inputs may be any that keep to these rules, and one draw needn't show every extreme that they name: `traces`: recorded samples.
All inputs are finite; a program needn't handle non-finite values. No bound on the sum of `live_mask` on one device may be relied on, other than what follows from the above.
Results may differ from the reference program's by a relative error of at most 0.015.
The reference program's roundings to bfloat16 on the way (of `table`, `spectra`, `rotated`, `filter_bf` and `error`) count: a program that leaves them out, or rounds other values in their place, can miss the bound.
Values may be sent and summed in bfloat16 or wider, within the bound.
No kernel may reach another device: no remote copies, remote signals or barrier semaphores. Data moves between devices by JAX's collectives and lax.ppermute only.
A program may use at most 128 MiB of HBM per device.

```python
import jax
import jax.numpy as jnp
from jax import lax

CHANNELS = 256
SAMPLES = 8192
LAGS = 4
FREQS = 512
CORR_LAGS = 8
SHOTS = 96


def draw_traces(key, part):
    subkeys = jax.random.split(jax.random.fold_in(key, 7), 8)
    source_count = 128
    noise_part = 0.3 * jax.random.normal(subkeys[0], (SHOTS, CHANNELS, SAMPLES), jnp.float32)
    band_edge = jnp.pi * FREQS / SAMPLES
    centre = band_edge * jax.random.uniform(subkeys[1], (source_count,), jnp.float32, 0.15, 0.95)
    radius = jax.random.uniform(subkeys[2], (source_count,), jnp.float32, 0.96, 0.995)
    first_coef = 2.0 * radius * jnp.cos(centre)
    second_coef = -radius * radius
    variance = (1.0 + radius * radius) / ((1.0 - radius * radius) * ((1.0 + radius * radius) ** 2 - first_coef * first_coef))
    drive_scale = 1.0 / jnp.sqrt(variance)

    def advance(carry, sample_idx):
        earlier, latest = carry
        innovation = jax.random.normal(jax.random.fold_in(subkeys[3], sample_idx), (SHOTS, source_count), jnp.float32)
        updated = first_coef * latest + second_coef * earlier + drive_scale * innovation
        return ((latest, updated), updated)
    start_state = (jnp.zeros((SHOTS, source_count), jnp.float32), jnp.zeros((SHOTS, source_count), jnp.float32))
    final_state, sources = lax.scan(advance, start_state, jnp.arange(SAMPLES, dtype=jnp.int32))
    amplitude = jnp.exp(-3.0 * jnp.log(10.0) * jax.random.uniform(subkeys[4], (source_count,), jnp.float32))
    mixing = jax.random.normal(subkeys[5], (CHANNELS, source_count), jnp.float32) * (0.3 * amplitude)[None, :]
    shot_ramp = 3.0 ** (jnp.arange(SHOTS, dtype=jnp.float32) / max(SHOTS - 1, 1))
    chan_scale = jnp.exp(jax.random.uniform(subkeys[6], (CHANNELS,), jnp.float32, jnp.log(0.5), jnp.log(5.0)))
    trace_scale = jax.random.uniform(subkeys[7], (SHOTS, CHANNELS), jnp.float32, 0.7, 1.3) * chan_scale[None, :]
    coherent = jnp.einsum('tsm,cm->sct', sources, mixing)
    recorded = (noise_part + coherent) * trace_scale[:, :, None] * shot_ramp[:, None, None]
    return jnp.clip(recorded, -64.0, 64.0).astype(jnp.bfloat16)


def set_ends(result, stream_key, low, largest):
    longest = result.shape.index(max(result.shape))
    spots = []
    for shift in (0, 1):
        where = [jax.random.randint(jax.random.fold_in(stream_key, axis), (), 0, length) for axis, length in enumerate(result.shape)]
        where[longest] = (where[longest] + shift) % result.shape[longest]
        spots.append(tuple(where))
    return result.at[spots[0]].set(low).at[spots[1]].set(largest)


def setup_inputs(seed: int = 0) -> dict:
    arg_keys = jax.random.split(jax.random.key(seed), 4)
    traces = draw_traces(jax.random.fold_in(arg_keys[3], 71), 0)
    live_mask = set_ends((jax.random.randint(arg_keys[1], (SHOTS, CHANNELS), 0, 8) < 7).astype(jnp.int32), jax.random.fold_in(arg_keys[1], 1), 0, 1)
    gap_samples = jax.random.randint(arg_keys[2], (1,), 1, 33).astype(jnp.int32)
    return {"traces": traces, "live_mask": live_mask, "gap_samples": gap_samples}


def dft_table(first_row, row_count, samples, band_size):
    times_idx = jnp.arange(row_count, dtype=jnp.int32) + first_row
    harmonic = jnp.arange(1, band_size + 1, dtype=jnp.int32)
    phase = times_idx[:, None] * harmonic[None, :] % (2 * samples)
    angle = phase.astype(jnp.float32) * (jnp.pi / samples)
    return jnp.concatenate([jnp.cos(angle), jnp.sin(angle)], axis=1).astype(jnp.bfloat16)

def delay_tables(delays, samples, band_size):
    harmonic = jnp.arange(1, band_size + 1, dtype=jnp.int32)
    phase = delays[:, None] * harmonic[None, :] % (2 * samples)
    angle = phase.astype(jnp.float32) * (jnp.pi / samples)
    return (jnp.cos(angle), jnp.sin(angle))

def delay_apply(spectrum, cosine, sine):
    band_size = cosine.shape[-1]
    real_part = spectrum[..., :band_size]
    imag_part = spectrum[..., band_size:]
    return jnp.concatenate([real_part * cosine - imag_part * sine, imag_part * cosine + real_part * sine], axis=-1)

def reference(traces, live_mask, gap_samples):
    table = dft_table(0, SAMPLES, SAMPLES, FREQS)
    spacing = SAMPLES // (2 * FREQS)
    tap_delays = jnp.arange(LAGS, dtype=jnp.int32) * spacing
    lag_list = jnp.concatenate([tap_delays, gap_samples[0].astype(jnp.int32) + tap_delays])
    cosine, sine = delay_tables(lag_list, SAMPLES, FREQS)
    live_bf = live_mask.astype(jnp.bfloat16)

    def spectrum_of(shot_idx):
        masked = traces[shot_idx] * live_bf[shot_idx][:, None]
        return jnp.dot(masked.astype(jnp.float32), table.astype(jnp.float32), preferred_element_type=jnp.float32).astype(jnp.bfloat16)
    spectra = lax.map(spectrum_of, jnp.arange(SHOTS, dtype=jnp.int32))

    def accumulate(carry, spectrum):
        rotated = delay_apply(spectrum.astype(jnp.float32)[None], cosine[:, None, :], sine[:, None, :]).astype(jnp.bfloat16)
        update = jnp.einsum('kaf,bf->kab', rotated.astype(jnp.float32), spectrum.astype(jnp.float32))
        return (carry + update, None)
    start_sum = jnp.zeros((CORR_LAGS, CHANNELS, CHANNELS), jnp.float32)
    summed, unused = lax.scan(accumulate, start_sum, spectra)
    correlation = summed * (1.0 / SAMPLES) * (1.0 / (SAMPLES * SHOTS))
    whiten = 0.1 * jnp.mean(jnp.diagonal(correlation[0])) + 1e-06
    zero_lag = correlation[0] + whiten * jnp.eye(CHANNELS, dtype=jnp.float32)
    weighted = jnp.concatenate([zero_lag[None], correlation[1:]], axis=0)
    blocks = []
    for row_block in range(LAGS):
        row_parts = []
        for col_block in range(LAGS):
            if row_block >= col_block:
                row_parts.append(weighted[row_block - col_block])
            else:
                row_parts.append(weighted[col_block - row_block].T)
        blocks.append(jnp.concatenate(row_parts, axis=1))
    system = jnp.concatenate(blocks, axis=0)
    rhs = jnp.concatenate([weighted[LAGS + row_block] for row_block in range(LAGS)], axis=0)
    lower_factor = jnp.linalg.cholesky(system)
    filter_all = jax.scipy.linalg.cho_solve((lower_factor, True), rhs)
    filter_bf = filter_all.astype(jnp.bfloat16).reshape(LAGS, CHANNELS, CHANNELS)

    def residual_of(shot_idx):
        spectrum = spectra[shot_idx]
        mixed = jnp.einsum('jab,af->jbf', filter_bf.astype(jnp.float32), spectrum.astype(jnp.float32))
        shifted = delay_apply(mixed, cosine[LAGS:, None, :], sine[LAGS:, None, :])
        error = (spectrum.astype(jnp.float32) - jnp.sum(shifted, axis=0)).astype(jnp.bfloat16)
        restored = jnp.dot(error.astype(jnp.float32), table.T.astype(jnp.float32), preferred_element_type=jnp.float32)
        return (restored * (1.0 / SAMPLES) * live_bf[shot_idx].astype(jnp.float32)[:, None]).astype(jnp.bfloat16)
    return lax.map(residual_of, jnp.arange(SHOTS, dtype=jnp.int32))
```

```python
import jax
import jax.numpy as jnp
from jax import lax
from jax.experimental import pallas as pl
from jax.experimental.pallas import tpu as pltpu
from jax.sharding import PartitionSpec as P

LAGS = 4
CHUNK = 1024
FINE = 128
f32 = jnp.float32
bf = jnp.bfloat16
VM = pl.BlockSpec(memory_space=pltpu.VMEM)


def wave(times, samples, band_size):
    harmonic = jnp.arange(1, band_size + 1, dtype=jnp.int32)
    phase = times[:, None] * harmonic[None, :] % (2 * samples)
    angle = phase.astype(f32) * (jnp.pi / samples)
    return jnp.cos(angle), jnp.sin(angle)

def forward_kernel(x_ref, live_ref, cc_ref, cs_ref, fc_ref, fs_ref, spec_ref, table_ref, acc):
    step = pl.program_id(0)
    chunk, width = table_ref.shape
    band = width // 2
    fine = fc_ref.shape[0]
    rows = acc.shape[0]
    for r in range(chunk // fine):
        h = step * (chunk // fine) + r
        cc = cc_ref[pl.ds(h, 1), :]
        cs = cs_ref[pl.ds(h, 1), :]
        at = slice(r * fine, (r + 1) * fine)
        table_ref[at, :band] = (cc * fc_ref[...] - cs * fs_ref[...]).astype(bf)
        table_ref[at, band:] = (cs * fc_ref[...] + cc * fs_ref[...]).astype(bf)
    part = jnp.dot(x_ref[...].reshape(rows, chunk), table_ref[...], preferred_element_type=f32)

    @pl.when(step == 0)
    def _():
        acc[...] = part

    @pl.when(step > 0)
    def _():
        acc[...] += part

    @pl.when(step == pl.num_programs(0) - 1)
    def _():
        spec_ref[...] = (acc[...] * live_ref[...]).astype(bf)

def forward(traces, live):
    shots, chans, samples = traces.shape
    band = samples // 16
    rows = shots * chans
    cc, cs = wave(jnp.arange(samples // FINE, dtype=jnp.int32) * FINE, samples, band)
    fc, fs = wave(jnp.arange(FINE, dtype=jnp.int32), samples, band)
    return pl.pallas_call(
        forward_kernel, grid=(samples // CHUNK,),
        out_shape=(jax.ShapeDtypeStruct((rows, 2 * band), bf), jax.ShapeDtypeStruct((samples, 2 * band), bf)),
        in_specs=[pl.BlockSpec((shots, chans, CHUNK), lambda i: (0, 0, i)), VM, VM, VM, VM, VM],
        out_specs=(pl.BlockSpec((rows, 2 * band), lambda i: (0, 0)), pl.BlockSpec((CHUNK, 2 * band), lambda i: (i, 0))),
        scratch_shapes=[pltpu.VMEM((rows, 2 * band), f32)],
        compiler_params=pltpu.CompilerParams(vmem_limit_bytes=40 * 2**20),
    )(traces, live.reshape(rows, 1), cc, cs, fc, fs)

def inverse_kernel(filter_ref, all_ref, own_ref, cos_ref, sin_ref, live_ref, table_ref, out_ref, error):
    shots, chans, chunk = out_ref.shape
    band = cos_ref.shape[1]

    @pl.when(pl.program_id(0) == 0)
    def _():
        weights = filter_ref[...].reshape(LAGS * chans, filter_ref.shape[2])
        for s in range(shots):
            mixed = jnp.dot(weights, all_ref[s], preferred_element_type=f32)
            even = jnp.zeros((chans, band), f32)
            odd = jnp.zeros((chans, band), f32)
            for j in range(LAGS):
                part = mixed[j * chans : (j + 1) * chans]
                c, n = cos_ref[j : j + 1, :], sin_ref[j : j + 1, :]
                even = even + (part[:, :band] * c - part[:, band:] * n)
                odd = odd + (part[:, band:] * c + part[:, :band] * n)
            at = slice(s * chans, (s + 1) * chans)
            error[at, :band] = (own_ref[at, :band].astype(f32) - even).astype(bf)
            error[at, band:] = (own_ref[at, band:].astype(f32) - odd).astype(bf)

    restored = lax.dot_general(error[...], table_ref[...], (((1,), (1,)), ((), ())), preferred_element_type=f32)
    samples = pl.num_programs(0) * chunk
    out_ref[...] = (restored * (1.0 / samples) * live_ref[...]).astype(bf).reshape(out_ref.shape)

def inverse(filter_bf, all_spec, own_spec, cosine, sine, live, table):
    shots, channels, width = all_spec.shape
    chans = filter_bf.shape[1]
    samples = table.shape[0]
    rows = shots * chans
    return pl.pallas_call(
        inverse_kernel, grid=(samples // CHUNK,),
        out_shape=jax.ShapeDtypeStruct((shots, chans, samples), bf),
        in_specs=[VM, VM, VM, VM, VM, VM, pl.BlockSpec((CHUNK, width), lambda i: (i, 0))],
        out_specs=pl.BlockSpec((shots, chans, CHUNK), lambda i: (0, 0, i)),
        scratch_shapes=[pltpu.VMEM((rows, width), bf)],
        compiler_params=pltpu.CompilerParams(vmem_limit_bytes=40 * 2**20),
    )(filter_bf, all_spec, own_spec, cosine, sine, live.reshape(rows, 1), table)


def delay_apply(spectrum, cosine, sine):
    band_size = cosine.shape[-1]
    real_part = spectrum[..., :band_size]
    imag_part = spectrum[..., band_size:]
    return jnp.concatenate(
        [real_part * cosine - imag_part * sine, imag_part * cosine + real_part * sine], axis=-1
    )


def invert_128(groups):
    lane = lax.broadcasted_iota(jnp.int32, (8, 128), 1)
    sub = lax.broadcasted_iota(jnp.int32, (8, 128), 0)
    groups = list(groups)
    for s in range(16):
        lo = 8 * s
        inside = (lane >= lo) & (lane < lo + 8)
        rows = groups[s]
        entry = {}
        for j in range(8):
            for i in range(j, 8):
                entry[i, j] = jnp.broadcast_to(rows[i:i+1, lo+j:lo+j+1], (8, 128))
        unit = jnp.where(lane - lo == sub, 1.0, 0.0)
        start = jnp.where(inside, unit, rows)
        y = [jnp.broadcast_to(start[j:j+1, :], (8, 128)) for j in range(8)]
        low = {}
        dinv = []
        for j in range(8):
            d = 1.0 / entry[j, j]
            dinv.append(d)
            for i in range(j + 1, 8):
                low[i, j] = entry[i, j] * d
            for i in range(j + 1, 8):
                for k in range(j + 1, i + 1):
                    entry[i, k] = entry[i, k] - low[i, j] * entry[k, j]
                y[i] = y[i] - low[i, j] * y[j]
        v = [None] * 8
        for j in reversed(range(8)):
            t = y[j] * dinv[j]
            for i in range(j + 1, 8):
                t = t - low[i, j] * v[i]
            v[j] = t
        order = [(s + 1 + g) % 16 for g in range(15)]
        for g in order:
            x = groups[g]
            t = jnp.where(inside, 0.0, x)
            for j in range(8):
                t = t - jnp.broadcast_to(x[:, lo+j:lo+j+1], (8, 128)) * v[j]
            groups[g] = t
        t = v[0]
        for j in range(1, 8):
            t = jnp.where(sub == j, v[j], t)
        groups[s] = t
    return groups


def mm(a, b, ca=1, cb=0):
    return lax.dot_general(a, b, (((ca,), (cb,)), ((), ())), precision=lax.Precision.HIGHEST, preferred_element_type=f32)

def solve_kernel(corr_ref, rhs_ref, out_ref, tiles, gains, ys, block, whole):
    n = corr_ref.shape[1]
    h = n // 2
    eye = lax.broadcasted_iota(jnp.int32, (n, n), 0) == lax.broadcasted_iota(jnp.int32, (n, n), 1)
    zero_lag = corr_ref[0]
    whiten = 0.1 * jnp.sum(jnp.where(eye, zero_lag, 0.0)) / n + 1e-06
    zero_lag = zero_lag + jnp.where(eye, whiten, 0.0)
    for i in range(LAGS):
        tiles[i, i] = zero_lag
        for j in range(i):
            tiles[i, j] = corr_ref[i - j]
        ys[i] = rhs_ref[i]
    block[...] = zero_lag[:h, :h]

    def first_half(p):
        inv = block[...]
        corner = tiles[p, p, h:, :h]
        left = mm(corner, inv)
        whole[:h, :h] = inv
        whole[h:, :h] = left
        block[...] = tiles[p, p, h:, h:] - mm(left, corner, 1, 1)

    def second_half(p):
        inv = block[...]
        left = whole[h:, :h]
        low = mm(inv, left)
        whole[:h, :h] += mm(left, low, 0, 0)
        whole[h:, :h] = -low
        whole[:h, h:] = -low.T
        whole[h:, h:] = inv
        full = whole[...]
        for i in range(p + 1, LAGS):
            gains[i, p] = mm(tiles[i, p], full)
            for j in range(p + 1, i + 1):
                tiles[i, j] -= mm(gains[i, p], tiles[j, p], 1, 1)
        if p + 1 < LAGS:
            block[...] = tiles[p + 1, p + 1, :h, :h]
        y = mm(ys[p], full)
        ys[p] = y
        for j in range(p + 1, LAGS):
            ys[j] -= mm(y, tiles[j, p], 1, 1)

    def step(q, carry):
        even = 0.5 * (block[...] + block[...].T)
        groups = invert_128([even[8 * i : 8 * i + 8, :] for i in range(16)])
        for i in range(16):
            block[8 * i : 8 * i + 8, :] = groups[i]
        for p in range(LAGS):
            pl.when(q == 2 * p)(lambda p=p: first_half(p))
            pl.when(q == 2 * p + 1)(lambda p=p: second_half(p))
        return carry

    lax.fori_loop(0, 2 * LAGS, step, 0)
    for p in reversed(range(LAGS)):
        x = ys[p]
        for j in range(p + 1, LAGS):
            x = x - mm(ys[j], gains[j, p])
        ys[p] = x
        out_ref[p] = x.astype(out_ref.dtype)

def solve_filter(corr, rhs):
    n = corr.shape[1]; m = rhs.shape[1]; h = n // 2
    vm = pl.BlockSpec(memory_space=pltpu.VMEM)
    return pl.pallas_call(solve_kernel, out_shape=jax.ShapeDtypeStruct((LAGS, m, n), jnp.bfloat16), in_specs=[vm, vm], out_specs=vm,
        scratch_shapes=[pltpu.VMEM((LAGS, LAGS, n, n), f32), pltpu.VMEM((LAGS, LAGS, n, n), f32), pltpu.VMEM((LAGS, m, n), f32), pltpu.VMEM((h, h), f32), pltpu.VMEM((n, n), f32)],
        compiler_params=pltpu.CompilerParams(vmem_limit_bytes=40 * 2**20))(corr, rhs)


def gather_all(x, axis):
    parts = lax.axis_size(axis)
    return lax.all_to_all(
        jnp.broadcast_to(x[None], (parts,) + x.shape), axis, split_axis=0, concat_axis=0, tiled=True
    )


def sum_over(x, axis):
    parts = lax.axis_size(axis)
    rows = x.shape[0] // parts
    split = x.reshape((parts, rows) + x.shape[1:])
    swapped = lax.all_to_all(split, axis, split_axis=0, concat_axis=0, tiled=True)
    return gather_all(jnp.sum(swapped, axis=0), axis).reshape(x.shape)


def shards(traces, live_mask, gap_samples):
    shot_count, local_chan, samples = traces.shape
    band_size = samples // 16
    live = live_mask.astype(f32)
    own_rows, table = forward(traces, live)
    own_spec = own_rows.reshape(shot_count, local_chan, 2 * band_size)
    all_spec = lax.all_gather(own_spec, "lag", axis=1, tiled=True)
    spacing = samples // (2 * band_size)
    tap_delays = jnp.arange(LAGS, dtype=jnp.int32) * spacing
    lag_list = jnp.concatenate([tap_delays, gap_samples[0] + tap_delays])
    cosine, sine = wave(lag_list, samples, band_size)
    turn = jnp.where(jnp.arange(2 * LAGS) < LAGS, 1.0, -1.0).astype(f32)[:, None]
    rotated = delay_apply(
        own_spec.astype(f32)[None], cosine[:, None, None, :], (turn * sine)[:, None, None, :]
    ).astype(jnp.bfloat16)
    partial_value = jnp.einsum("ksaf,sbf->kab", rotated, all_spec, preferred_element_type=f32)
    channels = all_spec.shape[1]
    total_shots = shot_count * lax.axis_size("shot")
    summed = sum_over(partial_value.reshape(2 * LAGS * local_chan, channels), "shot")
    summed = summed * (1.0 / samples) * (1.0 / (samples * total_shots))
    summed = summed.reshape(2 * LAGS, local_chan, channels)
    gathered = gather_all(summed[:LAGS], "lag")
    correlation = jnp.swapaxes(gathered, 0, 1).reshape(LAGS, channels, channels)
    filter_bf = solve_filter(correlation, summed[LAGS:])
    return inverse(filter_bf, all_spec, own_rows, cosine[LAGS:], sine[LAGS:], live, table)


def solution(mesh):
    placed = (P("shot", "lag", None), P("shot", "lag"), P())
    return jax.shard_map(
        shards, mesh=mesh, in_specs=placed, out_specs=P("shot", "lag", None), check_vma=False
    )
```

```python
import jax
import jax.numpy as jnp
from jax import lax
from jax.experimental import pallas as pl
from jax.experimental.pallas import tpu as pltpu
from jax.sharding import PartitionSpec as P

LAGS = 4
CHUNK = 1024
FINE = 128
f32 = jnp.float32
bf = jnp.bfloat16
VM = pl.BlockSpec(memory_space=pltpu.VMEM)


def wave(times, samples, band_size):
    harmonic = jnp.arange(1, band_size + 1, dtype=jnp.int32)
    phase = times[:, None] * harmonic[None, :] % (2 * samples)
    angle = phase.astype(f32) * (jnp.pi / samples)
    return jnp.cos(angle), jnp.sin(angle)

def forward_kernel(x_ref, live_ref, cc_ref, cs_ref, fc_ref, fs_ref, spec_ref, table_ref, acc):
    step = pl.program_id(0)
    chunk, width = table_ref.shape
    band = width // 2
    fine = fc_ref.shape[0]
    rows = acc.shape[0]
    for r in range(chunk // fine):
        h = step * (chunk // fine) + r
        cc = cc_ref[pl.ds(h, 1), :]
        cs = cs_ref[pl.ds(h, 1), :]
        at = slice(r * fine, (r + 1) * fine)
        table_ref[at, :band] = (cc * fc_ref[...] - cs * fs_ref[...]).astype(bf)
        table_ref[at, band:] = (cs * fc_ref[...] + cc * fs_ref[...]).astype(bf)
    part = jnp.dot(x_ref[...].reshape(rows, chunk), table_ref[...], preferred_element_type=f32)

    @pl.when(step == 0)
    def _():
        acc[...] = part

    @pl.when(step > 0)
    def _():
        acc[...] += part

    @pl.when(step == pl.num_programs(0) - 1)
    def _():
        spec_ref[...] = (acc[...] * live_ref[...]).astype(bf)

def forward(traces, live):
    shots, chans, samples = traces.shape
    band = samples // 16
    rows = shots * chans
    cc, cs = wave(jnp.arange(samples // FINE, dtype=jnp.int32) * FINE, samples, band)
    fc, fs = wave(jnp.arange(FINE, dtype=jnp.int32), samples, band)
    return pl.pallas_call(
        forward_kernel, grid=(samples // CHUNK,),
        out_shape=(jax.ShapeDtypeStruct((rows, 2 * band), bf), jax.ShapeDtypeStruct((samples, 2 * band), bf)),
        in_specs=[pl.BlockSpec((shots, chans, CHUNK), lambda i: (0, 0, i)), VM, VM, VM, VM, VM],
        out_specs=(pl.BlockSpec((rows, 2 * band), lambda i: (0, 0)), pl.BlockSpec((CHUNK, 2 * band), lambda i: (i, 0))),
        scratch_shapes=[pltpu.VMEM((rows, 2 * band), f32)],
        compiler_params=pltpu.CompilerParams(vmem_limit_bytes=40 * 2**20),
    )(traces, live.reshape(rows, 1), cc, cs, fc, fs)

def inverse_kernel(order_ref, filter_ref, own_ref, cos_ref, sin_ref, live_ref, table_ref, *refs):
    *piece_refs, out_ref, error, full = refs
    shots, chans, chunk = out_ref.shape
    band = cos_ref.shape[1]

    @pl.when(pl.program_id(0) == 0)
    def _():
        weights = filter_ref[...].reshape(LAGS * chans, filter_ref.shape[2])
        for s in range(shots):
            place(order_ref, piece_refs, s, full)
            mixed = jnp.dot(weights, full[...], preferred_element_type=f32)
            even = jnp.zeros((chans, band), f32)
            odd = jnp.zeros((chans, band), f32)
            for j in range(LAGS):
                part = mixed[j * chans : (j + 1) * chans]
                c, n = cos_ref[j : j + 1, :], sin_ref[j : j + 1, :]
                even = even + (part[:, :band] * c - part[:, band:] * n)
                odd = odd + (part[:, band:] * c + part[:, :band] * n)
            at = slice(s * chans, (s + 1) * chans)
            error[at, :band] = (own_ref[at, :band].astype(f32) - even).astype(bf)
            error[at, band:] = (own_ref[at, band:].astype(f32) - odd).astype(bf)

    restored = lax.dot_general(error[...], table_ref[...], (((1,), (1,)), ((), ())), preferred_element_type=f32)
    samples = pl.num_programs(0) * chunk
    out_ref[...] = (restored * (1.0 / samples) * live_ref[...]).astype(bf).reshape(out_ref.shape)

def inverse(order, filter_bf, pieces, own_rows, cosine, sine, live, table):
    shots, chans = live.shape
    rows, width = own_rows.shape
    samples = table.shape[0]
    channels = filter_bf.shape[2]
    return pl.pallas_call(
        inverse_kernel,
        grid=(samples // CHUNK,),
        out_shape=jax.ShapeDtypeStruct((shots, chans, samples), bf),
        in_specs=[pl.BlockSpec(memory_space=pltpu.SMEM)]
        + [VM] * 5
        + [pl.BlockSpec((CHUNK, width), lambda i: (i, 0))]
        + [VM] * len(pieces),
        out_specs=pl.BlockSpec((shots, chans, CHUNK), lambda i: (0, 0, i)),
        scratch_shapes=[pltpu.VMEM((rows, width), bf), pltpu.VMEM((channels, width), bf)],
        compiler_params=pltpu.CompilerParams(vmem_limit_bytes=40 * 2**20),
    )(order, filter_bf, own_rows, cosine, sine, live.reshape(rows, 1), table, *pieces)


def invert_128(groups, spare):
    lane = lax.broadcasted_iota(jnp.int32, (8, 128), 1)
    sub = lax.broadcasted_iota(jnp.int32, (8, 128), 0)
    groups = list(groups)
    for s in range(16):
        lo = 8 * s
        inside = (lane >= lo) & (lane < lo + 8)
        rows = groups[s]
        unit = jnp.where(lane - lo == sub, 1.0, 0.0)
        for j in range(8):
            spare[s % 2, j] = jnp.broadcast_to(rows[:, lo + j : lo + j + 1], (8, 128))
        spare[s % 2, 8] = jnp.where(inside, unit, rows)
        entry = {
            (i, j): jnp.broadcast_to(spare[s % 2, j, i : i + 1, :], (8, 128))
            for j in range(8)
            for i in range(j, 8)
        }
        y = [jnp.broadcast_to(spare[s % 2, 8, j : j + 1, :], (8, 128)) for j in range(8)]
        low = {}
        dinv = []
        for j in range(8):
            d = 1.0 / entry[j, j]
            dinv.append(d)
            for i in range(j + 1, 8):
                low[i, j] = entry[i, j] * d
            for i in range(j + 1, 8):
                for k in range(j + 1, i + 1):
                    entry[i, k] = entry[i, k] - low[i, j] * entry[k, j]
                y[i] = y[i] - low[i, j] * y[j]
        v = [None] * 8
        for j in reversed(range(8)):
            t = y[j] * dinv[j]
            for i in range(j + 1, 8):
                t = t - low[i, j] * v[i]
            v[j] = t
        order = [(s + 1 + g) % 16 for g in range(15)]
        for g in order:
            x = groups[g]
            t = jnp.where(inside, 0.0, x)
            for j in range(8):
                t = t - jnp.broadcast_to(x[:, lo+j:lo+j+1], (8, 128)) * v[j]
            groups[g] = t
        t = v[0]
        for j in range(1, 8):
            t = jnp.where(sub == j, v[j], t)
        groups[s] = t
    return groups


def mm(a, b, ca=1, cb=0):
    return lax.dot_general(a, b, (((ca,), (cb,)), ((), ())), precision=lax.Precision.HIGHEST, preferred_element_type=f32)

def solve_kernel(order_ref, rhs_ref, *refs):
    *piece_refs, out_ref, corr_ref, tiles, gains, ys, block, whole, spare = refs
    n = corr_ref.shape[1]
    for k in range(LAGS):
        place(order_ref, piece_refs, k, corr_ref.at[k])
    h = n // 2
    eye = lax.broadcasted_iota(jnp.int32, (n, n), 0) == lax.broadcasted_iota(jnp.int32, (n, n), 1)
    zero_lag = corr_ref[0]
    whiten = 0.1 * jnp.sum(jnp.where(eye, zero_lag, 0.0)) / n + 1e-06
    zero_lag = zero_lag + jnp.where(eye, whiten, 0.0)
    for i in range(LAGS):
        tiles[i, i] = zero_lag
        for j in range(i):
            tiles[i, j] = corr_ref[i - j]
        ys[i] = rhs_ref[i]
    block[...] = zero_lag[:h, :h]

    def first_half(p):
        inv = block[...]
        corner = tiles[p, p, h:, :h]
        left = mm(corner, inv)
        whole[:h, :h] = inv
        whole[h:, :h] = left
        block[...] = tiles[p, p, h:, h:] - mm(left, corner, 1, 1)

    def second_half(p):
        inv = block[...]
        left = whole[h:, :h]
        low = mm(inv, left)
        whole[:h, :h] += mm(left, low, 0, 0)
        whole[h:, :h] = -low
        whole[:h, h:] = -low.T
        whole[h:, h:] = inv
        full = whole[...]
        for i in range(p + 1, LAGS):
            gains[i, p] = mm(tiles[i, p], full)
            for j in range(p + 1, i + 1):
                tiles[i, j] -= mm(gains[i, p], tiles[j, p], 1, 1)
        if p + 1 < LAGS:
            block[...] = tiles[p + 1, p + 1, :h, :h]
        y = mm(ys[p], full)
        ys[p] = y
        for j in range(p + 1, LAGS):
            ys[j] -= mm(y, tiles[j, p], 1, 1)

    def step(q, carry):
        even = 0.5 * (block[...] + block[...].T)
        groups = invert_128([even[8 * i : 8 * i + 8, :] for i in range(16)], spare)
        for i in range(16):
            block[8 * i : 8 * i + 8, :] = groups[i]
        for p in range(LAGS):
            pl.when(q == 2 * p)(lambda p=p: first_half(p))
            pl.when(q == 2 * p + 1)(lambda p=p: second_half(p))
        return carry

    lax.fori_loop(0, 2 * LAGS, step, 0)
    for p in reversed(range(LAGS)):
        x = ys[p]
        for j in range(p + 1, LAGS):
            x = x - mm(ys[j], gains[j, p])
        ys[p] = x
        out_ref[p] = x.astype(out_ref.dtype)

def solve_filter(order, pieces, rhs):
    chans = rhs.shape[1]
    n = rhs.shape[2]
    half = n // 2
    return pl.pallas_call(
        solve_kernel,
        out_shape=jax.ShapeDtypeStruct((LAGS, chans, n), bf),
        in_specs=[pl.BlockSpec(memory_space=pltpu.SMEM)] + [VM] * (1 + len(pieces)),
        out_specs=VM,
        scratch_shapes=[
            pltpu.VMEM((LAGS, n, n), f32),
            pltpu.VMEM((LAGS, LAGS, n, n), f32),
            pltpu.VMEM((LAGS, LAGS, n, n), f32),
            pltpu.VMEM((LAGS, chans, n), f32),
            pltpu.VMEM((half, half), f32),
            pltpu.VMEM((n, n), f32),
            pltpu.VMEM((2, 9, 8, half), f32),
        ],
        compiler_params=pltpu.CompilerParams(vmem_limit_bytes=40 * 2**20),
    )(order, rhs, *pieces)


def place(order_ref, piece_refs, shot, full):
    count = 0
    for ref in piece_refs:
        for i in range(ref.shape[0]):
            rows = ref.shape[2]
            full[pl.ds(pl.multiple_of(order_ref[count] * rows, rows), rows), :] = ref[i, shot]
            count += 1


def correlate_kernel(order_ref, own_ref, cos_ref, sin_ref, *refs):
    *piece_refs, out_ref, rotated, full = refs
    shots = piece_refs[0].shape[1]
    chans = piece_refs[0].shape[2]
    band = cos_ref.shape[1]
    for s in range(shots):
        place(order_ref, piece_refs, s, full)
        even = own_ref[s * chans : (s + 1) * chans, :band].astype(f32)
        odd = own_ref[s * chans : (s + 1) * chans, band:].astype(f32)
        for k in range(2 * LAGS):
            c, n = cos_ref[k : k + 1, :], sin_ref[k : k + 1, :]
            at = slice(k * chans, (k + 1) * chans)
            rotated[at, :band] = (even * c - odd * n).astype(bf)
            rotated[at, band:] = (odd * c + even * n).astype(bf)
        part = lax.dot_general(
            rotated[...], full[...], (((1,), (1,)), ((), ())), preferred_element_type=f32
        )
        if s == 0:
            out_ref[...] = part
        else:
            out_ref[...] += part


def correlate(order, own_rows, cosine, sine, pieces):
    width = own_rows.shape[1]
    chans = pieces[0].shape[2]
    channels = chans * order.shape[0]
    rows = 2 * LAGS * chans
    return pl.pallas_call(
        correlate_kernel,
        out_shape=jax.ShapeDtypeStruct((rows, channels), f32),
        in_specs=[pl.BlockSpec(memory_space=pltpu.SMEM)] + [VM] * (3 + len(pieces)),
        out_specs=VM,
        scratch_shapes=[pltpu.VMEM((rows, width), bf), pltpu.VMEM((channels, width), bf)],
        compiler_params=pltpu.CompilerParams(vmem_limit_bytes=40 * 2**20),
    )(order, own_rows, cosine, sine, *pieces)


def lag_moves():
    def move(dx, dy, dc):
        return [
            ((x * 4 + y) * 2 + c, ((x ^ dx) * 4 + (y + dy) % 4) * 2 + (c ^ dc))
            for x in range(2)
            for y in range(4)
            for c in range(2)
        ]

    return move(1, 0, 0), move(0, 1, 0), move(0, -1, 0), move(0, 0, 1)


def gather_lag(value):
    over_x, up, down, over_core = lag_moves()
    own = value[None]
    pair = jnp.concatenate([own, lax.ppermute(own, "lag", over_x)], axis=0)
    below = lax.ppermute(pair, "lag", up)
    above = lax.ppermute(pair, "lag", down)
    far_own = lax.ppermute(below[:1], "lag", up)
    far_other = lax.ppermute(above[1:], "lag", down)
    near = [pair, below, above, far_own, far_other]
    return near + [lax.ppermute(piece, "lag", over_core) for piece in near]


def lag_order():
    index = lax.axis_index("lag")
    x, y, core = index // 8, index // 2 % 4, index % 2
    places = [
        (x ^ dx) * 8 + (y + dy) % 4 * 2 + (core ^ dc)
        for dc in (0, 1)
        for dx, dy in ((0, 0), (1, 0), (0, 3), (1, 3), (0, 1), (1, 1), (0, 2), (1, 2))
    ]
    return jnp.stack(places).astype(jnp.int32)


def gather_all(x, axis):
    parts = lax.axis_size(axis)
    return lax.all_to_all(
        jnp.broadcast_to(x[None], (parts,) + x.shape), axis, split_axis=0, concat_axis=0, tiled=True
    )


def sum_over(x, axis):
    parts = lax.axis_size(axis)
    rows = x.shape[0] // parts
    split = x.reshape((parts, rows) + x.shape[1:])
    swapped = lax.all_to_all(split, axis, split_axis=0, concat_axis=0, tiled=True)
    return gather_all(jnp.sum(swapped, axis=0), axis).reshape(x.shape)


def shards(traces, live_mask, gap_samples):
    shot_count, local_chan, samples = traces.shape
    band_size = samples // 16
    live = live_mask.astype(f32)
    own_rows, table = forward(traces, live)
    own_spec = own_rows.reshape(shot_count, local_chan, 2 * band_size)
    order = lag_order()
    spectra = gather_lag(own_spec)
    spacing = samples // (2 * band_size)
    tap_delays = jnp.arange(LAGS, dtype=jnp.int32) * spacing
    lag_list = jnp.concatenate([tap_delays, gap_samples[0] + tap_delays])
    cosine, sine = wave(lag_list, samples, band_size)
    turn = jnp.where(jnp.arange(2 * LAGS) < LAGS, 1.0, -1.0).astype(f32)[:, None]
    partial_value = correlate(order, own_rows, cosine, turn * sine, spectra)
    channels = partial_value.shape[1]
    total_shots = shot_count * lax.axis_size("shot")
    summed = sum_over(partial_value, "shot")
    summed = summed * (1.0 / samples) * (1.0 / (samples * total_shots))
    summed = summed.reshape(2 * LAGS, local_chan, channels)
    correlation = gather_lag(summed[:LAGS])
    filter_bf = solve_filter(order, correlation, summed[LAGS:])
    return inverse(order, filter_bf, spectra, own_rows, cosine[LAGS:], sine[LAGS:], live, table)


def solution(mesh):
    placed = (P("shot", "lag", None), P("shot", "lag"), P())
    return jax.shard_map(
        shards, mesh=mesh, in_specs=placed, out_specs=P("shot", "lag", None), check_vma=False
    )
```

```python
import jax
import jax.numpy as jnp
from jax import lax
from jax.experimental import pallas as pl
from jax.experimental.pallas import tpu as pltpu
from jax.sharding import PartitionSpec as P

LAGS = 4
CHUNK = 1024
FINE = 128
f32 = jnp.float32
bf = jnp.bfloat16
VM = pl.BlockSpec(memory_space=pltpu.VMEM)


def wave(times, samples, band_size):
    harmonic = jnp.arange(1, band_size + 1, dtype=jnp.int32)
    phase = times[:, None] * harmonic[None, :] % (2 * samples)
    angle = phase.astype(f32) * (jnp.pi / samples)
    return jnp.cos(angle), jnp.sin(angle)

def forward_kernel(x_ref, live_ref, cc_ref, cs_ref, fc_ref, fs_ref, spec_ref, table_ref, acc):
    step = pl.program_id(0)
    chunk, width = table_ref.shape
    band = width // 2
    fine = fc_ref.shape[0]
    rows = acc.shape[0]
    for r in range(chunk // fine):
        h = step * (chunk // fine) + r
        cc = cc_ref[pl.ds(h, 1), :]
        cs = cs_ref[pl.ds(h, 1), :]
        at = slice(r * fine, (r + 1) * fine)
        table_ref[at, :band] = (cc * fc_ref[...] - cs * fs_ref[...]).astype(bf)
        table_ref[at, band:] = (cs * fc_ref[...] + cc * fs_ref[...]).astype(bf)
    part = jnp.dot(x_ref[...].reshape(rows, chunk), table_ref[...], preferred_element_type=f32)

    @pl.when(step == 0)
    def _():
        acc[...] = part

    @pl.when(step > 0)
    def _():
        acc[...] += part

    @pl.when(step == pl.num_programs(0) - 1)
    def _():
        spec_ref[...] = (acc[...] * live_ref[...]).astype(bf)

def forward(traces, live):
    shots, chans, samples = traces.shape
    band = samples // 16
    rows = shots * chans
    cc, cs = wave(jnp.arange(samples // FINE, dtype=jnp.int32) * FINE, samples, band)
    fc, fs = wave(jnp.arange(FINE, dtype=jnp.int32), samples, band)
    return pl.pallas_call(
        forward_kernel, grid=(samples // CHUNK,),
        out_shape=(jax.ShapeDtypeStruct((rows, 2 * band), bf), jax.ShapeDtypeStruct((samples, 2 * band), bf)),
        in_specs=[pl.BlockSpec((shots, chans, CHUNK), lambda i: (0, 0, i)), VM, VM, VM, VM, VM],
        out_specs=(pl.BlockSpec((rows, 2 * band), lambda i: (0, 0)), pl.BlockSpec((CHUNK, 2 * band), lambda i: (i, 0))),
        scratch_shapes=[pltpu.VMEM((rows, 2 * band), f32)],
        compiler_params=pltpu.CompilerParams(vmem_limit_bytes=40 * 2**20),
    )(traces, live.reshape(rows, 1), cc, cs, fc, fs)

def inverse_kernel(order_ref, filter_ref, own_ref, cos_ref, sin_ref, live_ref, table_ref, *refs):
    *piece_refs, out_ref, error, full = refs
    shots, chans, chunk = out_ref.shape
    band = cos_ref.shape[1]

    @pl.when(pl.program_id(0) == 0)
    def _():
        weights = filter_ref[...].reshape(LAGS * chans, filter_ref.shape[2])
        for s in range(shots):
            place(order_ref, piece_refs, s, full)
            mixed = jnp.dot(weights, full[...], preferred_element_type=f32)
            even = jnp.zeros((chans, band), f32)
            odd = jnp.zeros((chans, band), f32)
            for j in range(LAGS):
                part = mixed[j * chans : (j + 1) * chans]
                c, n = cos_ref[j : j + 1, :], sin_ref[j : j + 1, :]
                even = even + (part[:, :band] * c - part[:, band:] * n)
                odd = odd + (part[:, band:] * c + part[:, :band] * n)
            at = slice(s * chans, (s + 1) * chans)
            error[at, :band] = (own_ref[at, :band].astype(f32) - even).astype(bf)
            error[at, band:] = (own_ref[at, band:].astype(f32) - odd).astype(bf)

    restored = lax.dot_general(error[...], table_ref[...], (((1,), (1,)), ((), ())), preferred_element_type=f32)
    samples = pl.num_programs(0) * chunk
    out_ref[...] = (restored * (1.0 / samples) * live_ref[...]).astype(bf).reshape(out_ref.shape)

def inverse(order, filter_bf, pieces, own_rows, cosine, sine, live, table):
    shots, chans = live.shape
    rows, width = own_rows.shape
    samples = table.shape[0]
    channels = filter_bf.shape[2]
    return pl.pallas_call(
        inverse_kernel,
        grid=(samples // CHUNK,),
        out_shape=jax.ShapeDtypeStruct((shots, chans, samples), bf),
        in_specs=[pl.BlockSpec(memory_space=pltpu.SMEM)]
        + [VM] * 5
        + [pl.BlockSpec((CHUNK, width), lambda i: (i, 0))]
        + [VM] * len(pieces),
        out_specs=pl.BlockSpec((shots, chans, CHUNK), lambda i: (0, 0, i)),
        scratch_shapes=[pltpu.VMEM((rows, width), bf), pltpu.VMEM((channels, width), bf)],
        compiler_params=pltpu.CompilerParams(vmem_limit_bytes=40 * 2**20),
    )(order, filter_bf, own_rows, cosine, sine, live.reshape(rows, 1), table, *pieces)


def invert_128(groups, spare):
    lane = lax.broadcasted_iota(jnp.int32, (8, 128), 1)
    sub = lax.broadcasted_iota(jnp.int32, (8, 128), 0)
    groups = list(groups)
    for s in range(16):
        lo = 8 * s
        inside = (lane >= lo) & (lane < lo + 8)
        rows = groups[s]
        unit = jnp.where(lane - lo == sub, 1.0, 0.0)
        for j in range(8):
            spare[s % 2, j] = jnp.broadcast_to(rows[:, lo + j : lo + j + 1], (8, 128))
        spare[s % 2, 8] = jnp.where(inside, unit, rows)
        entry = {
            (i, j): jnp.broadcast_to(spare[s % 2, j, i : i + 1, :], (8, 128))
            for j in range(8)
            for i in range(j, 8)
        }
        y = [jnp.broadcast_to(spare[s % 2, 8, j : j + 1, :], (8, 128)) for j in range(8)]
        low = {}
        dinv = []
        for j in range(8):
            d = 1.0 / entry[j, j]
            dinv.append(d)
            for i in range(j + 1, 8):
                low[i, j] = entry[i, j] * d
            for i in range(j + 1, 8):
                for k in range(j + 1, i + 1):
                    entry[i, k] = entry[i, k] - low[i, j] * entry[k, j]
                y[i] = y[i] - low[i, j] * y[j]
        v = [None] * 8
        for j in reversed(range(8)):
            t = y[j] * dinv[j]
            for i in range(j + 1, 8):
                t = t - low[i, j] * v[i]
            v[j] = t
        order = [(s + 1 + g) % 16 for g in range(15)]
        for g in order:
            x = groups[g]
            t = jnp.where(inside, 0.0, x)
            for j in range(8):
                t = t - jnp.broadcast_to(x[:, lo+j:lo+j+1], (8, 128)) * v[j]
            groups[g] = t
        t = v[0]
        for j in range(1, 8):
            t = jnp.where(sub == j, v[j], t)
        groups[s] = t
    return groups


def mm(a, b, ca=1, cb=0):
    return lax.dot_general(a, b, (((ca,), (cb,)), ((), ())), precision=lax.Precision.HIGHEST, preferred_element_type=f32)

def solve_kernel(order_ref, rhs_ref, *refs):
    *piece_refs, out_ref, corr_ref, tiles, gains, ys, block, whole, spare = refs
    n = corr_ref.shape[1]
    for k in range(LAGS):
        place(order_ref, piece_refs, k, corr_ref.at[k])
    h = n // 2
    eye = lax.broadcasted_iota(jnp.int32, (n, n), 0) == lax.broadcasted_iota(jnp.int32, (n, n), 1)
    zero_lag = corr_ref[0]
    whiten = 0.1 * jnp.sum(jnp.where(eye, zero_lag, 0.0)) / n + 1e-06
    zero_lag = zero_lag + jnp.where(eye, whiten, 0.0)
    for i in range(LAGS):
        tiles[i, i] = zero_lag
        for j in range(i):
            tiles[i, j] = corr_ref[i - j]
        ys[i] = rhs_ref[i]
    block[...] = zero_lag[:h, :h]

    def first_half(p):
        inv = block[...]
        corner = tiles[p, p, h:, :h]
        left = mm(corner, inv)
        whole[:h, :h] = inv
        whole[h:, :h] = left
        block[...] = tiles[p, p, h:, h:] - mm(left, corner, 1, 1)

    def second_half(p):
        inv = block[...]
        left = whole[h:, :h]
        low = mm(inv, left)
        whole[:h, :h] += mm(left, low, 0, 0)
        whole[h:, :h] = -low
        whole[:h, h:] = -low.T
        whole[h:, h:] = inv
        full = whole[...]
        for i in range(p + 1, LAGS):
            gains[i, p] = mm(tiles[i, p], full)
            for j in range(p + 1, i + 1):
                tiles[i, j] -= mm(gains[i, p], tiles[j, p], 1, 1)
        if p + 1 < LAGS:
            block[...] = tiles[p + 1, p + 1, :h, :h]
        y = mm(ys[p], full)
        ys[p] = y
        for j in range(p + 1, LAGS):
            ys[j] -= mm(y, tiles[j, p], 1, 1)

    def step(q, carry):
        even = 0.5 * (block[...] + block[...].T)
        groups = invert_128([even[8 * i : 8 * i + 8, :] for i in range(16)], spare)
        for i in range(16):
            block[8 * i : 8 * i + 8, :] = groups[i]
        for p in range(LAGS):
            pl.when(q == 2 * p)(lambda p=p: first_half(p))
            pl.when(q == 2 * p + 1)(lambda p=p: second_half(p))
        return carry

    lax.fori_loop(0, 2 * LAGS, step, 0)
    for p in reversed(range(LAGS)):
        x = ys[p]
        for j in range(p + 1, LAGS):
            x = x - mm(ys[j], gains[j, p])
        ys[p] = x
        out_ref[p] = x.astype(out_ref.dtype)

def solve_filter(order, pieces, rhs):
    chans = rhs.shape[1]
    n = rhs.shape[2]
    half = n // 2
    return pl.pallas_call(
        solve_kernel,
        out_shape=jax.ShapeDtypeStruct((LAGS, chans, n), bf),
        in_specs=[pl.BlockSpec(memory_space=pltpu.SMEM)] + [VM] * (1 + len(pieces)),
        out_specs=VM,
        scratch_shapes=[
            pltpu.VMEM((LAGS, n, n), f32),
            pltpu.VMEM((LAGS, LAGS, n, n), f32),
            pltpu.VMEM((LAGS, LAGS, n, n), f32),
            pltpu.VMEM((LAGS, chans, n), f32),
            pltpu.VMEM((half, half), f32),
            pltpu.VMEM((n, n), f32),
            pltpu.VMEM((2, 9, 8, half), f32),
        ],
        compiler_params=pltpu.CompilerParams(vmem_limit_bytes=40 * 2**20),
    )(order, rhs, *pieces)


def place(order_ref, piece_refs, shot, full):
    count = 0
    for ref in piece_refs:
        for i in range(ref.shape[0]):
            rows = ref.shape[2]
            full[pl.ds(pl.multiple_of(order_ref[count] * rows, rows), rows), :] = ref[i, shot]
            count += 1


def correlate_kernel(order_ref, own_ref, cos_ref, sin_ref, *refs):
    *piece_refs, out_ref, rotated, full = refs
    shots = piece_refs[0].shape[1]
    chans = piece_refs[0].shape[2]
    band = cos_ref.shape[1]
    for s in range(shots):
        place(order_ref, piece_refs, s, full)
        even = own_ref[s * chans : (s + 1) * chans, :band].astype(f32)
        odd = own_ref[s * chans : (s + 1) * chans, band:].astype(f32)
        for k in range(2 * LAGS):
            c, n = cos_ref[k : k + 1, :], sin_ref[k : k + 1, :]
            at = slice(k * chans, (k + 1) * chans)
            rotated[at, :band] = (even * c - odd * n).astype(bf)
            rotated[at, band:] = (odd * c + even * n).astype(bf)
        part = lax.dot_general(
            rotated[...], full[...], (((1,), (1,)), ((), ())), preferred_element_type=f32
        )
        if s == 0:
            out_ref[...] = part
        else:
            out_ref[...] += part


def correlate(order, own_rows, cosine, sine, pieces):
    width = own_rows.shape[1]
    chans = pieces[0].shape[2]
    channels = chans * order.shape[0]
    rows = 2 * LAGS * chans
    return pl.pallas_call(
        correlate_kernel,
        out_shape=jax.ShapeDtypeStruct((rows, channels), f32),
        in_specs=[pl.BlockSpec(memory_space=pltpu.SMEM)] + [VM] * (3 + len(pieces)),
        out_specs=VM,
        scratch_shapes=[pltpu.VMEM((rows, width), bf), pltpu.VMEM((channels, width), bf)],
        compiler_params=pltpu.CompilerParams(vmem_limit_bytes=40 * 2**20),
    )(order, own_rows, cosine, sine, *pieces)


def lag_moves():
    def move(dx, dy, dc):
        return [
            ((x * 4 + y) * 2 + c, ((x ^ dx) * 4 + (y + dy) % 4) * 2 + (c ^ dc))
            for x in range(2)
            for y in range(4)
            for c in range(2)
        ]

    return move(1, 0, 0), move(0, 1, 0), move(0, -1, 0), move(0, 0, 1)


def gather_lag(value):
    over_x, up, down, over_core = lag_moves()
    own = value[None]
    pair = jnp.concatenate([own, lax.ppermute(own, "lag", over_x)], axis=0)
    below = lax.ppermute(pair, "lag", up)
    above = lax.ppermute(pair, "lag", down)
    far_own = lax.ppermute(below[:1], "lag", up)
    far_other = lax.ppermute(above[1:], "lag", down)
    near = [pair, below, above, far_own, far_other]
    return near + [lax.ppermute(piece, "lag", over_core) for piece in near]


def lag_order():
    index = lax.axis_index("lag")
    x, y, core = index // 8, index // 2 % 4, index % 2
    places = [
        (x ^ dx) * 8 + (y + dy) % 4 * 2 + (core ^ dc)
        for dc in (0, 1)
        for dx, dy in ((0, 0), (1, 0), (0, 3), (1, 3), (0, 1), (1, 1), (0, 2), (1, 2))
    ]
    return jnp.stack(places).astype(jnp.int32)


def gather_all(x, axis):
    parts = lax.axis_size(axis)
    return lax.all_to_all(
        jnp.broadcast_to(x[None], (parts,) + x.shape), axis, split_axis=0, concat_axis=0, tiled=True
    )


def sum_over_shot(value):
    for bit in (8, 1, 2, 4):
        pairs = [(i, i ^ bit) for i in range(16)]
        value = value + lax.ppermute(value, "shot", pairs)
    return value


def shards(traces, live_mask, gap_samples):
    shot_count, local_chan, samples = traces.shape
    band_size = samples // 16
    live = live_mask.astype(f32)
    own_rows, table = forward(traces, live)
    own_spec = own_rows.reshape(shot_count, local_chan, 2 * band_size)
    order = lag_order()
    spectra = gather_lag(own_spec)
    spacing = samples // (2 * band_size)
    tap_delays = jnp.arange(LAGS, dtype=jnp.int32) * spacing
    lag_list = jnp.concatenate([tap_delays, gap_samples[0] + tap_delays])
    cosine, sine = wave(lag_list, samples, band_size)
    turn = jnp.where(jnp.arange(2 * LAGS) < LAGS, 1.0, -1.0).astype(f32)[:, None]
    partial_value = correlate(order, own_rows, cosine, turn * sine, spectra)
    channels = partial_value.shape[1]
    total_shots = shot_count * lax.axis_size("shot")
    scale = (1.0 / samples) * (1.0 / (samples * total_shots))
    half = LAGS * local_chan
    targets = jnp.sum(gather_all(partial_value[half:], "shot"), axis=0) * scale
    summed = sum_over_shot(partial_value[:half]) * scale
    correlation = gather_lag(summed.reshape(LAGS, local_chan, channels))
    filter_bf = solve_filter(order, correlation, targets.reshape(LAGS, local_chan, channels))
    return inverse(order, filter_bf, spectra, own_rows, cosine[LAGS:], sine[LAGS:], live, table)


def solution(mesh):
    placed = (P("shot", "lag", None), P("shot", "lag"), P())
    return jax.shard_map(
        shards, mesh=mesh, in_specs=placed, out_specs=P("shot", "lag", None), check_vma=False
    )
```

```python
import jax
import jax.numpy as jnp
from jax import lax
from jax.experimental import pallas as pl
from jax.experimental.pallas import tpu as pltpu
from jax.sharding import PartitionSpec as P

LAGS = 4
CHUNK = 2048
BACK_CHUNK = 4096
FINE = 128
f32 = jnp.float32
bf = jnp.bfloat16
VM = pl.BlockSpec(memory_space=pltpu.VMEM)


def wave(times, samples, band_size):
    harmonic = jnp.arange(1, band_size + 1, dtype=jnp.int32)
    phase = times[:, None] * harmonic[None, :] % (2 * samples)
    angle = phase.astype(f32) * (jnp.pi / samples)
    return jnp.cos(angle), jnp.sin(angle)

def quarter_turn(even, odd, sign):
    turn = (lax.broadcasted_iota(jnp.int32, even.shape, 1) + 1) % 4
    cross = jnp.where(turn == 1, sign, jnp.where(turn == 3, -sign, 0.0)).astype(f32)
    along = jnp.where(turn == 0, 1.0, jnp.where(turn == 2, -1.0, 0.0)).astype(f32)
    return even * along - odd * cross, odd * along + even * cross


def forward_kernel(early_ref, late_ref, live_ref, cc_ref, cs_ref, fc_ref, fs_ref, spec_ref, table_ref, acc):
    step = pl.program_id(0)
    chunk, width = table_ref.shape
    band = width // 2
    fine = fc_ref.shape[0]
    rows = spec_ref.shape[0]
    for r in range(chunk // fine):
        h = step * (chunk // fine) + r
        cc = cc_ref[pl.ds(h, 1), :]
        cs = cs_ref[pl.ds(h, 1), :]
        at = slice(r * fine, (r + 1) * fine)
        table_ref[at, :band] = (cc * fc_ref[...] - cs * fs_ref[...]).astype(bf)
        table_ref[at, band:] = (cs * fc_ref[...] + cc * fs_ref[...]).astype(bf)
    both = jnp.concatenate(
        [early_ref[...].reshape(rows, chunk), late_ref[...].reshape(rows, chunk)], axis=0
    )
    part = jnp.dot(both, table_ref[...], preferred_element_type=f32)

    @pl.when(step == 0)
    def _():
        acc[...] = part

    @pl.when(step > 0)
    def _():
        acc[...] += part

    @pl.when(step == pl.num_programs(0) - 1)
    def _():
        even, odd = quarter_turn(acc[rows:, :band], acc[rows:, band:], 1.0)
        spec_ref[:, :band] = ((acc[:rows, :band] + even) * live_ref[...]).astype(bf)
        spec_ref[:, band:] = ((acc[:rows, band:] + odd) * live_ref[...]).astype(bf)


def forward(traces, live):
    shots, chans, samples = traces.shape
    band = samples // 16
    rows = shots * chans
    steps = samples // 2 // CHUNK
    cc, cs = wave(jnp.arange(samples // 2 // FINE, dtype=jnp.int32) * FINE, samples, band)
    fc, fs = wave(jnp.arange(FINE, dtype=jnp.int32), samples, band)
    return pl.pallas_call(
        forward_kernel,
        grid=(steps,),
        out_shape=(
            jax.ShapeDtypeStruct((rows, 2 * band), bf),
            jax.ShapeDtypeStruct((samples // 2, 2 * band), bf),
        ),
        in_specs=[
            pl.BlockSpec((shots, chans, CHUNK), lambda i: (0, 0, i)),
            pl.BlockSpec((shots, chans, CHUNK), lambda i: (0, 0, i + steps)),
        ]
        + [VM] * 5,
        out_specs=(
            pl.BlockSpec((rows, 2 * band), lambda i: (0, 0)),
            pl.BlockSpec((CHUNK, 2 * band), lambda i: (i, 0)),
        ),
        scratch_shapes=[pltpu.VMEM((2 * rows, 2 * band), f32)],
        compiler_params=pltpu.CompilerParams(vmem_limit_bytes=40 * 2**20),
    )(traces, traces, live.reshape(rows, 1), cc, cs, fc, fs)


def inverse_kernel(order_ref, filter_ref, own_ref, cos_ref, sin_ref, live_ref, table_ref, *refs):
    *piece_refs, out_ref, error, full, later = refs
    half = pl.program_id(1)
    rows = own_ref.shape[0]
    shots, chans, chunk = out_ref.shape
    band = cos_ref.shape[1]

    @pl.when((pl.program_id(0) == 0) & (half == 0))
    def _():
        weights = filter_ref[...].reshape(LAGS * chans, filter_ref.shape[2])
        for s in range(shots):
            place(order_ref, piece_refs, s, full)
            mixed = jnp.dot(weights, full[...], preferred_element_type=f32)
            even = jnp.zeros((chans, band), f32)
            odd = jnp.zeros((chans, band), f32)
            for j in range(LAGS):
                part = mixed[j * chans : (j + 1) * chans]
                c, n = cos_ref[j : j + 1, :], sin_ref[j : j + 1, :]
                even = even + (part[:, :band] * c - part[:, band:] * n)
                odd = odd + (part[:, band:] * c + part[:, :band] * n)
            at = slice(s * chans, (s + 1) * chans)
            error[at, :band] = (own_ref[at, :band].astype(f32) - even).astype(bf)
            error[at, band:] = (own_ref[at, band:].astype(f32) - odd).astype(bf)

        turned = quarter_turn(error[:rows, :band].astype(f32), error[:rows, band:].astype(f32), -1.0)
        error[rows:, :band] = turned[0].astype(bf)
        error[rows:, band:] = turned[1].astype(bf)

    samples = 2 * pl.num_programs(0) * chunk

    @pl.when(half == 0)
    def _():
        restored = lax.dot_general(
            error[...], table_ref[...], (((1,), (1,)), ((), ())), preferred_element_type=f32
        )
        later[...] = (restored[rows:] * (1.0 / samples) * live_ref[...]).astype(bf)
        out_ref[...] = (restored[:rows] * (1.0 / samples) * live_ref[...]).astype(bf).reshape(out_ref.shape)

    @pl.when(half == 1)
    def _():
        out_ref[...] = later[...].reshape(out_ref.shape)


def inverse(order, filter_bf, pieces, own_rows, cosine, sine, live, table):
    shots, chans = live.shape
    rows, width = own_rows.shape
    samples = 2 * table.shape[0]
    steps = table.shape[0] // BACK_CHUNK
    channels = filter_bf.shape[2]
    return pl.pallas_call(
        inverse_kernel,
        grid=(steps, 2),
        out_shape=jax.ShapeDtypeStruct((shots, chans, samples), bf),
        in_specs=[pl.BlockSpec(memory_space=pltpu.SMEM)]
        + [VM] * 5
        + [pl.BlockSpec((BACK_CHUNK, width), lambda i, h: (i, 0))]
        + [VM] * len(pieces),
        out_specs=pl.BlockSpec((shots, chans, BACK_CHUNK), lambda i, h: (0, 0, i + h * steps)),
        scratch_shapes=[
            pltpu.VMEM((2 * rows, width), bf),
            pltpu.VMEM((channels, width), bf),
            pltpu.VMEM((rows, BACK_CHUNK), bf),
        ],
        compiler_params=pltpu.CompilerParams(vmem_limit_bytes=40 * 2**20),
    )(order, filter_bf, own_rows, cosine, sine, live.reshape(rows, 1), table, *pieces)


def invert_128(groups, spare):
    lane = lax.broadcasted_iota(jnp.int32, (8, 128), 1)
    sub = lax.broadcasted_iota(jnp.int32, (8, 128), 0)
    groups = list(groups)
    for s in range(16):
        lo = 8 * s
        inside = (lane >= lo) & (lane < lo + 8)
        rows = groups[s]
        unit = jnp.where(lane - lo == sub, 1.0, 0.0)
        for j in range(8):
            spare[s % 2, j] = jnp.broadcast_to(rows[:, lo + j : lo + j + 1], (8, 128))
        spare[s % 2, 8] = jnp.where(inside, unit, rows)
        entry = {
            (i, j): jnp.broadcast_to(spare[s % 2, j, i : i + 1, :], (8, 128))
            for j in range(8)
            for i in range(j, 8)
        }
        y = [jnp.broadcast_to(spare[s % 2, 8, j : j + 1, :], (8, 128)) for j in range(8)]
        low = {}
        dinv = []
        for j in range(8):
            d = 1.0 / entry[j, j]
            dinv.append(d)
            for i in range(j + 1, 8):
                low[i, j] = entry[i, j] * d
            for i in range(j + 1, 8):
                for k in range(j + 1, i + 1):
                    entry[i, k] = entry[i, k] - low[i, j] * entry[k, j]
                y[i] = y[i] - low[i, j] * y[j]
        v = [None] * 8
        for j in reversed(range(8)):
            t = y[j] * dinv[j]
            for i in range(j + 1, 8):
                t = t - low[i, j] * v[i]
            v[j] = t
        order = [(s + 1 + g) % 16 for g in range(15)]
        for g in order:
            x = groups[g]
            t = jnp.where(inside, 0.0, x)
            for j in range(8):
                t = t - jnp.broadcast_to(x[:, lo+j:lo+j+1], (8, 128)) * v[j]
            groups[g] = t
        t = v[0]
        for j in range(1, 8):
            t = jnp.where(sub == j, v[j], t)
        groups[s] = t
    return groups


def mm(a, b, ca=1, cb=0):
    return lax.dot_general(a, b, (((ca,), (cb,)), ((), ())), precision=lax.Precision.HIGHEST, preferred_element_type=f32)

def solve_kernel(order_ref, rhs_ref, *refs):
    *piece_refs, out_ref, columns, gains, block, whole, spare = refs
    chans, n = rhs_ref.shape[1:]
    h = n // 2
    end = LAGS * n + chans
    count = 0
    for ref in piece_refs:
        for i in range(ref.shape[0]):
            start = pl.multiple_of(order_ref[count] * chans, chans)
            for k in range(LAGS):
                for j in range(LAGS - k):
                    columns[j, pl.ds((j + k) * n + start, chans), :] = ref[i, k]
            count += 1
    for j in range(LAGS):
        columns[j, LAGS * n :, :] = rhs_ref[j]
    row = lax.broadcasted_iota(jnp.int32, (n, n), 0)
    eye = row == lax.broadcasted_iota(jnp.int32, (n, n), 1)
    whiten = 0.1 * jnp.sum(jnp.where(eye, columns[0, :n], 0.0)) / n + 1e-06
    whiten = jnp.where(eye[:h, :h], whiten, 0.0)
    block[...] = columns[0, :h, :h] + whiten

    def first_half(p):
        inv = block[...]
        corner = columns[p, p * n + h : (p + 1) * n, :h]
        left = mm(corner, inv)
        whole[:h, :h] = inv
        whole[h:, :h] = left
        block[...] = columns[p, p * n + h : (p + 1) * n, h:] + whiten - mm(left, corner, 1, 1)

    def second_half(p):
        inv = block[...]
        left = whole[h:, :h]
        low = mm(inv, left)
        whole[:h, :h] += mm(left, low, 0, 0)
        whole[h:, :h] = -low
        whole[:h, h:] = -low.T
        whole[h:, h:] = inv
        below = (p + 1) * n
        gain = mm(columns[p, below:, :], whole[...])
        gains[p, below:, :] = gain
        for j in range(p + 1, LAGS):
            columns[j, j * n :, :] -= mm(gain[j * n - below :], columns[p, j * n : (j + 1) * n, :], 1, 1)
        if p + 1 < LAGS:
            block[...] = columns[p + 1, below : below + h, :h] + whiten

    def step(q, carry):
        even = 0.5 * (block[...] + block[...].T)
        groups = invert_128([even[8 * i : 8 * i + 8, :] for i in range(16)], spare)
        for i in range(16):
            block[8 * i : 8 * i + 8, :] = groups[i]
        for p in range(LAGS):
            pl.when(q == 2 * p)(lambda p=p: first_half(p))
            pl.when(q == 2 * p + 1)(lambda p=p: second_half(p))
        return carry

    lax.fori_loop(0, 2 * LAGS, step, 0)
    solved = {}
    for p in reversed(range(LAGS)):
        x = gains[p, LAGS * n : end, :]
        for j in range(p + 1, LAGS):
            x = x - mm(solved[j], gains[p, j * n : (j + 1) * n, :])
        solved[p] = x
        out_ref[p] = x.astype(out_ref.dtype)


def solve_filter(order, pieces, rhs):
    chans = rhs.shape[1]
    n = rhs.shape[2]
    half = n // 2
    return pl.pallas_call(
        solve_kernel,
        out_shape=jax.ShapeDtypeStruct((LAGS, chans, n), bf),
        in_specs=[pl.BlockSpec(memory_space=pltpu.SMEM)] + [VM] * (1 + len(pieces)),
        out_specs=VM,
        scratch_shapes=[
            pltpu.VMEM((LAGS, LAGS * n + chans, n), f32),
            pltpu.VMEM((LAGS, LAGS * n + chans, n), f32),
            pltpu.VMEM((half, half), f32),
            pltpu.VMEM((n, n), f32),
            pltpu.VMEM((2, 9, 8, half), f32),
        ],
        compiler_params=pltpu.CompilerParams(vmem_limit_bytes=40 * 2**20),
    )(order, rhs, *pieces)


def place(order_ref, piece_refs, shot, full):
    count = 0
    for ref in piece_refs:
        for i in range(ref.shape[0]):
            rows = ref.shape[2]
            full[pl.ds(pl.multiple_of(order_ref[count] * rows, rows), rows), :] = ref[i, shot]
            count += 1


def correlate_kernel(order_ref, own_ref, cos_ref, sin_ref, *refs):
    *piece_refs, out_ref, rotated, full = refs
    shots = piece_refs[0].shape[1]
    chans = piece_refs[0].shape[2]
    band = cos_ref.shape[1]
    for s in range(shots):
        place(order_ref, piece_refs, s, full)
        even = own_ref[s * chans : (s + 1) * chans, :band].astype(f32)
        odd = own_ref[s * chans : (s + 1) * chans, band:].astype(f32)
        for k in range(2 * LAGS):
            c, n = cos_ref[k : k + 1, :], sin_ref[k : k + 1, :]
            at = slice(k * chans, (k + 1) * chans)
            rotated[at, :band] = (even * c - odd * n).astype(bf)
            rotated[at, band:] = (odd * c + even * n).astype(bf)
        part = lax.dot_general(
            rotated[...], full[...], (((1,), (1,)), ((), ())), preferred_element_type=f32
        )
        if s == 0:
            out_ref[...] = part
        else:
            out_ref[...] += part


def correlate(order, own_rows, cosine, sine, pieces):
    width = own_rows.shape[1]
    chans = pieces[0].shape[2]
    channels = chans * order.shape[0]
    rows = 2 * LAGS * chans
    return pl.pallas_call(
        correlate_kernel,
        out_shape=jax.ShapeDtypeStruct((rows, channels), f32),
        in_specs=[pl.BlockSpec(memory_space=pltpu.SMEM)] + [VM] * (3 + len(pieces)),
        out_specs=VM,
        scratch_shapes=[pltpu.VMEM((rows, width), bf), pltpu.VMEM((channels, width), bf)],
        compiler_params=pltpu.CompilerParams(vmem_limit_bytes=40 * 2**20),
    )(order, own_rows, cosine, sine, *pieces)


def lag_moves():
    def move(dx, dy, dc):
        return [
            ((x * 4 + y) * 2 + c, ((x ^ dx) * 4 + (y + dy) % 4) * 2 + (c ^ dc))
            for x in range(2)
            for y in range(4)
            for c in range(2)
        ]

    return move(1, 0, 0), move(0, 1, 0), move(0, -1, 0), move(0, 0, 1)


def gather_lag(value):
    over_x, up, down, over_core = lag_moves()
    own = value[None]
    pair = jnp.concatenate([own, lax.ppermute(own, "lag", over_x)], axis=0)
    below = lax.ppermute(pair, "lag", up)
    above = lax.ppermute(pair, "lag", down)
    far_own = lax.ppermute(below[:1], "lag", up)
    far_other = lax.ppermute(above[1:], "lag", down)
    near = [pair, below, above, far_own, far_other]
    return near + [lax.ppermute(piece, "lag", over_core) for piece in near]


def lag_order():
    index = lax.axis_index("lag")
    x, y, core = index // 8, index // 2 % 4, index % 2
    places = [
        (x ^ dx) * 8 + (y + dy) % 4 * 2 + (core ^ dc)
        for dc in (0, 1)
        for dx, dy in ((0, 0), (1, 0), (0, 3), (1, 3), (0, 1), (1, 1), (0, 2), (1, 2))
    ]
    return jnp.stack(places).astype(jnp.int32)


def sum_over_shot(value):
    for bit in (8, 1, 2, 4):
        pairs = [(i, i ^ bit) for i in range(16)]
        value = value + lax.ppermute(value, "shot", pairs)
    return value


def shards(traces, live_mask, gap_samples):
    shot_count, local_chan, samples = traces.shape
    band_size = samples // 16
    live = live_mask.astype(f32)
    own_rows, table = forward(traces, live)
    own_spec = own_rows.reshape(shot_count, local_chan, 2 * band_size)
    order = lag_order()
    spectra = gather_lag(own_spec)
    spacing = samples // (2 * band_size)
    tap_delays = jnp.arange(LAGS, dtype=jnp.int32) * spacing
    lag_list = jnp.concatenate([tap_delays, gap_samples[0] + tap_delays])
    cosine, sine = wave(lag_list, samples, band_size)
    turn = jnp.where(jnp.arange(2 * LAGS) < LAGS, 1.0, -1.0).astype(f32)[:, None]
    partial_value = correlate(order, own_rows, cosine, turn * sine, spectra)
    channels = partial_value.shape[1]
    total_shots = shot_count * lax.axis_size("shot")
    scale = (1.0 / samples) * (1.0 / (samples * total_shots))
    summed = sum_over_shot(partial_value) * scale
    summed = summed.reshape(2 * LAGS, local_chan, channels)
    correlation = gather_lag(summed[:LAGS])
    filter_bf = solve_filter(order, correlation, summed[LAGS:])
    return inverse(order, filter_bf, spectra, own_rows, cosine[LAGS:], sine[LAGS:], live, table)


def solution(mesh):
    placed = (P("shot", "lag", None), P("shot", "lag"), P())
    return jax.shard_map(
        shards, mesh=mesh, in_specs=placed, out_specs=P("shot", "lag", None), check_vma=False
    )
```

```python
import jax
import jax.numpy as jnp
from jax import lax
from jax.experimental import pallas as pl
from jax.experimental.pallas import tpu as pltpu
from jax.sharding import PartitionSpec as P

LAGS = 4
CHUNK = 4096
BACK_CHUNK = 4096
FINE = 128
f32 = jnp.float32
bf = jnp.bfloat16
VM = pl.BlockSpec(memory_space=pltpu.VMEM)


def wave(times, samples, band_size):
    harmonic = jnp.arange(1, band_size + 1, dtype=jnp.int32)
    phase = times[:, None] * harmonic[None, :] % (2 * samples)
    angle = phase.astype(f32) * (jnp.pi / samples)
    return jnp.cos(angle), jnp.sin(angle)

def quarter_turn(even, odd, sign):
    turn = (lax.broadcasted_iota(jnp.int32, even.shape, 1) + 1) % 4
    cross = jnp.where(turn == 1, sign, jnp.where(turn == 3, -sign, 0.0)).astype(f32)
    along = jnp.where(turn == 0, 1.0, jnp.where(turn == 2, -1.0, 0.0)).astype(f32)
    return even * along - odd * cross, odd * along + even * cross


def fill_table(step, wave_refs, table_ref):
    cc_ref, cs_ref, fc_ref, fs_ref = wave_refs
    fine, band = fc_ref.shape
    count = table_ref.shape[0] // fine
    for r in range(count):
        cc = cc_ref[pl.ds(step * count + r, 1), :]
        cs = cs_ref[pl.ds(step * count + r, 1), :]
        at = slice(r * fine, (r + 1) * fine)
        table_ref[at, :band] = (cc * fc_ref[...] - cs * fs_ref[...]).astype(bf)
        table_ref[at, band:] = (cs * fc_ref[...] + cc * fs_ref[...]).astype(bf)


def forward_kernel(early_ref, late_ref, live_ref, cc_ref, cs_ref, fc_ref, fs_ref, spec_ref, acc, table_ref):
    step = pl.program_id(0)
    chunk, width = table_ref.shape
    band = width // 2
    rows = spec_ref.shape[0]
    fill_table(step, (cc_ref, cs_ref, fc_ref, fs_ref), table_ref)
    both = jnp.concatenate(
        [early_ref[...].reshape(rows, chunk), late_ref[...].reshape(rows, chunk)], axis=0
    )
    part = jnp.dot(both, table_ref[...], preferred_element_type=f32)

    @pl.when(step == 0)
    def _():
        acc[...] = part

    @pl.when(step > 0)
    def _():
        acc[...] += part

    @pl.when(step == pl.num_programs(0) - 1)
    def _():
        even, odd = quarter_turn(acc[rows:, :band], acc[rows:, band:], 1.0)
        spec_ref[:, :band] = ((acc[:rows, :band] + even) * live_ref[...]).astype(bf)
        spec_ref[:, band:] = ((acc[:rows, band:] + odd) * live_ref[...]).astype(bf)


def forward(traces, live, waves):
    shots, chans, samples = traces.shape
    band = samples // 16
    rows = shots * chans
    steps = samples // 2 // CHUNK
    return pl.pallas_call(
        forward_kernel,
        grid=(steps,),
        out_shape=jax.ShapeDtypeStruct((rows, 2 * band), bf),
        in_specs=[
            pl.BlockSpec((shots, chans, CHUNK), lambda i: (0, 0, i)),
            pl.BlockSpec((shots, chans, CHUNK), lambda i: (0, 0, i + steps)),
        ]
        + [VM] * 5,
        out_specs=pl.BlockSpec((rows, 2 * band), lambda i: (0, 0)),
        scratch_shapes=[pltpu.VMEM((2 * rows, 2 * band), f32), pltpu.VMEM((CHUNK, 2 * band), bf)],
        compiler_params=pltpu.CompilerParams(vmem_limit_bytes=40 * 2**20),
    )(traces, traces, live.reshape(rows, 1), *waves)


def inverse_kernel(order_ref, filter_ref, own_ref, cos_ref, sin_ref, live_ref, *refs):
    wave_refs = refs[:4]
    *piece_refs, out_ref, error, full, later, table_ref = refs[4:]
    half = pl.program_id(1)
    rows = own_ref.shape[0]
    shots, chans, chunk = out_ref.shape
    band = cos_ref.shape[1]

    @pl.when((pl.program_id(0) == 0) & (half == 0))
    def _():
        weights = filter_ref[...].reshape(LAGS * chans, filter_ref.shape[2])
        for s in range(shots):
            place(order_ref, piece_refs, s, full)
            mixed = jnp.dot(weights, full[...], preferred_element_type=f32)
            even = jnp.zeros((chans, band), f32)
            odd = jnp.zeros((chans, band), f32)
            for j in range(LAGS):
                part = mixed[j * chans : (j + 1) * chans]
                c, n = cos_ref[j : j + 1, :], sin_ref[j : j + 1, :]
                even = even + (part[:, :band] * c - part[:, band:] * n)
                odd = odd + (part[:, band:] * c + part[:, :band] * n)
            at = slice(s * chans, (s + 1) * chans)
            error[at, :band] = (own_ref[at, :band].astype(f32) - even).astype(bf)
            error[at, band:] = (own_ref[at, band:].astype(f32) - odd).astype(bf)

        turned = quarter_turn(error[:rows, :band].astype(f32), error[:rows, band:].astype(f32), -1.0)
        error[rows:, :band] = turned[0].astype(bf)
        error[rows:, band:] = turned[1].astype(bf)

    samples = 2 * pl.num_programs(0) * chunk

    @pl.when(half == 0)
    def _():
        fill_table(pl.program_id(0), wave_refs, table_ref)
        restored = lax.dot_general(
            error[...], table_ref[...], (((1,), (1,)), ((), ())), preferred_element_type=f32
        )
        later[...] = (restored[rows:] * (1.0 / samples) * live_ref[...]).astype(bf)
        out_ref[...] = (restored[:rows] * (1.0 / samples) * live_ref[...]).astype(bf).reshape(out_ref.shape)

    @pl.when(half == 1)
    def _():
        out_ref[...] = later[...].reshape(out_ref.shape)


def inverse(order, filter_bf, pieces, own_rows, cosine, sine, live, waves, samples):
    shots, chans = live.shape
    rows, width = own_rows.shape
    steps = samples // 2 // BACK_CHUNK
    channels = filter_bf.shape[2]
    return pl.pallas_call(
        inverse_kernel,
        grid=(steps, 2),
        out_shape=jax.ShapeDtypeStruct((shots, chans, samples), bf),
        in_specs=[pl.BlockSpec(memory_space=pltpu.SMEM)]
        + [VM] * (9 + len(pieces)),
        out_specs=pl.BlockSpec((shots, chans, BACK_CHUNK), lambda i, h: (0, 0, i + h * steps)),
        scratch_shapes=[
            pltpu.VMEM((2 * rows, width), bf),
            pltpu.VMEM((channels, width), bf),
            pltpu.VMEM((rows, BACK_CHUNK), bf),
            pltpu.VMEM((BACK_CHUNK, width), bf),
        ],
        compiler_params=pltpu.CompilerParams(vmem_limit_bytes=40 * 2**20),
    )(order, filter_bf, own_rows, cosine, sine, live.reshape(rows, 1), *waves, *pieces)


def invert_128(groups, spare):
    lane = lax.broadcasted_iota(jnp.int32, (8, 128), 1)
    sub = lax.broadcasted_iota(jnp.int32, (8, 128), 0)
    groups = list(groups)
    for s in range(16):
        lo = 8 * s
        inside = (lane >= lo) & (lane < lo + 8)
        rows = groups[s]
        unit = jnp.where(lane - lo == sub, 1.0, 0.0)
        for j in range(8):
            spare[s % 2, j] = jnp.broadcast_to(rows[:, lo + j : lo + j + 1], (8, 128))
        spare[s % 2, 8] = jnp.where(inside, unit, rows)
        entry = {
            (i, j): jnp.broadcast_to(spare[s % 2, j, i : i + 1, :], (8, 128))
            for j in range(8)
            for i in range(j, 8)
        }
        y = [jnp.broadcast_to(spare[s % 2, 8, j : j + 1, :], (8, 128)) for j in range(8)]
        low = {}
        dinv = []
        for j in range(8):
            d = 1.0 / entry[j, j]
            dinv.append(d)
            for i in range(j + 1, 8):
                low[i, j] = entry[i, j] * d
            for i in range(j + 1, 8):
                for k in range(j + 1, i + 1):
                    entry[i, k] = entry[i, k] - low[i, j] * entry[k, j]
                y[i] = y[i] - low[i, j] * y[j]
        v = [None] * 8
        for j in reversed(range(8)):
            t = y[j] * dinv[j]
            for i in range(j + 1, 8):
                t = t - low[i, j] * v[i]
            v[j] = t
        order = [(s + 1 + g) % 16 for g in range(15)]
        for g in order:
            x = groups[g]
            t = jnp.where(inside, 0.0, x)
            for j in range(8):
                t = t - jnp.broadcast_to(x[:, lo+j:lo+j+1], (8, 128)) * v[j]
            groups[g] = t
        t = v[0]
        for j in range(1, 8):
            t = jnp.where(sub == j, v[j], t)
        groups[s] = t
    return groups


def mm(a, b, ca=1, cb=0):
    return lax.dot_general(a, b, (((ca,), (cb,)), ((), ())), precision=lax.Precision.HIGHEST, preferred_element_type=f32)

def solve_kernel(order_ref, rhs_ref, *refs):
    *piece_refs, out_ref, columns, gains, block, whole, spare = refs
    chans, n = rhs_ref.shape[1:]
    h = n // 2
    end = LAGS * n + chans
    count = 0
    for ref in piece_refs:
        for i in range(ref.shape[0]):
            start = pl.multiple_of(order_ref[count] * chans, chans)
            for k in range(LAGS):
                for j in range(LAGS - k):
                    columns[j, pl.ds((j + k) * n + start, chans), :] = ref[i, k]
            count += 1
    for j in range(LAGS):
        columns[j, LAGS * n :, :] = rhs_ref[j]
    row = lax.broadcasted_iota(jnp.int32, (n, n), 0)
    eye = row == lax.broadcasted_iota(jnp.int32, (n, n), 1)
    whiten = 0.1 * jnp.sum(jnp.where(eye, columns[0, :n], 0.0)) / n + 1e-06
    whiten = jnp.where(eye[:h, :h], whiten, 0.0)
    block[...] = columns[0, :h, :h] + whiten

    def first_half(p):
        inv = block[...]
        corner = columns[p, p * n + h : (p + 1) * n, :h]
        left = mm(corner, inv)
        whole[:h, :h] = inv
        whole[h:, :h] = left
        block[...] = columns[p, p * n + h : (p + 1) * n, h:] + whiten - mm(left, corner, 1, 1)

    def second_half(p):
        inv = block[...]
        left = whole[h:, :h]
        low = mm(inv, left)
        whole[:h, :h] += mm(left, low, 0, 0)
        whole[h:, :h] = -low
        whole[:h, h:] = -low.T
        whole[h:, h:] = inv
        below = (p + 1) * n
        gain = mm(columns[p, below:, :], whole[...])
        gains[p, below:, :] = gain
        for j in range(p + 1, LAGS):
            columns[j, j * n :, :] -= mm(gain[j * n - below :], columns[p, j * n : (j + 1) * n, :], 1, 1)
        if p + 1 < LAGS:
            block[...] = columns[p + 1, below : below + h, :h] + whiten

    def step(q, carry):
        even = 0.5 * (block[...] + block[...].T)
        groups = invert_128([even[8 * i : 8 * i + 8, :] for i in range(16)], spare)
        for i in range(16):
            block[8 * i : 8 * i + 8, :] = groups[i]
        for p in range(LAGS):
            pl.when(q == 2 * p)(lambda p=p: first_half(p))
            pl.when(q == 2 * p + 1)(lambda p=p: second_half(p))
        return carry

    lax.fori_loop(0, 2 * LAGS, step, 0)
    solved = {}
    for p in reversed(range(LAGS)):
        x = gains[p, LAGS * n : end, :]
        for j in range(p + 1, LAGS):
            x = x - mm(solved[j], gains[p, j * n : (j + 1) * n, :])
        solved[p] = x
        out_ref[p] = x.astype(out_ref.dtype)


def solve_filter(order, pieces, rhs):
    chans = rhs.shape[1]
    n = rhs.shape[2]
    half = n // 2
    return pl.pallas_call(
        solve_kernel,
        out_shape=jax.ShapeDtypeStruct((LAGS, chans, n), bf),
        in_specs=[pl.BlockSpec(memory_space=pltpu.SMEM)] + [VM] * (1 + len(pieces)),
        out_specs=VM,
        scratch_shapes=[
            pltpu.VMEM((LAGS, LAGS * n + chans, n), f32),
            pltpu.VMEM((LAGS, LAGS * n + chans, n), f32),
            pltpu.VMEM((half, half), f32),
            pltpu.VMEM((n, n), f32),
            pltpu.VMEM((2, 9, 8, half), f32),
        ],
        compiler_params=pltpu.CompilerParams(vmem_limit_bytes=40 * 2**20),
    )(order, rhs, *pieces)


def place(order_ref, piece_refs, shot, full):
    count = 0
    for ref in piece_refs:
        for i in range(ref.shape[0]):
            rows = ref.shape[2]
            full[pl.ds(pl.multiple_of(order_ref[count] * rows, rows), rows), :] = ref[i, shot]
            count += 1


def correlate_kernel(order_ref, own_ref, cos_ref, sin_ref, *refs):
    *piece_refs, out_ref, rotated, full = refs
    shots = piece_refs[0].shape[1]
    chans = piece_refs[0].shape[2]
    band = cos_ref.shape[1]
    for s in range(shots):
        place(order_ref, piece_refs, s, full)
        even = own_ref[s * chans : (s + 1) * chans, :band].astype(f32)
        odd = own_ref[s * chans : (s + 1) * chans, band:].astype(f32)
        for k in range(2 * LAGS):
            c, n = cos_ref[k : k + 1, :], sin_ref[k : k + 1, :]
            at = slice(k * chans, (k + 1) * chans)
            rotated[at, :band] = (even * c - odd * n).astype(bf)
            rotated[at, band:] = (odd * c + even * n).astype(bf)
        part = lax.dot_general(
            rotated[...], full[...], (((1,), (1,)), ((), ())), preferred_element_type=f32
        )
        if s == 0:
            out_ref[...] = part
        else:
            out_ref[...] += part


def correlate(order, own_rows, cosine, sine, pieces):
    width = own_rows.shape[1]
    chans = pieces[0].shape[2]
    channels = chans * order.shape[0]
    rows = 2 * LAGS * chans
    return pl.pallas_call(
        correlate_kernel,
        out_shape=jax.ShapeDtypeStruct((rows, channels), f32),
        in_specs=[pl.BlockSpec(memory_space=pltpu.SMEM)] + [VM] * (3 + len(pieces)),
        out_specs=VM,
        scratch_shapes=[pltpu.VMEM((rows, width), bf), pltpu.VMEM((channels, width), bf)],
        compiler_params=pltpu.CompilerParams(vmem_limit_bytes=40 * 2**20),
    )(order, own_rows, cosine, sine, *pieces)


def lag_moves():
    def move(dx, dy, dc):
        return [
            ((x * 4 + y) * 2 + c, ((x ^ dx) * 4 + (y + dy) % 4) * 2 + (c ^ dc))
            for x in range(2)
            for y in range(4)
            for c in range(2)
        ]

    return move(1, 0, 0), move(0, 1, 0), move(0, -1, 0), move(0, 0, 1)


def gather_lag(value):
    over_x, up, down, over_core = lag_moves()
    own = value[None]
    pair = jnp.concatenate([own, lax.ppermute(own, "lag", over_x)], axis=0)
    below = lax.ppermute(pair, "lag", up)
    above = lax.ppermute(pair, "lag", down)
    far_own = lax.ppermute(below[:1], "lag", up)
    far_other = lax.ppermute(above[1:], "lag", down)
    near = [pair, below, above, far_own, far_other]
    return near + [lax.ppermute(piece, "lag", over_core) for piece in near]


def lag_order():
    index = lax.axis_index("lag")
    x, y, core = index // 8, index // 2 % 4, index % 2
    places = [
        (x ^ dx) * 8 + (y + dy) % 4 * 2 + (core ^ dc)
        for dc in (0, 1)
        for dx, dy in ((0, 0), (1, 0), (0, 3), (1, 3), (0, 1), (1, 1), (0, 2), (1, 2))
    ]
    return jnp.stack(places).astype(jnp.int32)


def sum_over_shot(value):
    for bit in (8, 1, 2, 4):
        pairs = [(i, i ^ bit) for i in range(16)]
        value = value + lax.ppermute(value, "shot", pairs)
    return value


def shards(traces, live_mask, gap_samples):
    shot_count, local_chan, samples = traces.shape
    band_size = samples // 16
    live = live_mask.astype(f32)
    coarse = jnp.arange(samples // 2 // FINE, dtype=jnp.int32) * FINE
    waves = wave(coarse, samples, band_size) + wave(jnp.arange(FINE, dtype=jnp.int32), samples, band_size)
    own_rows = forward(traces, live, waves)
    own_spec = own_rows.reshape(shot_count, local_chan, 2 * band_size)
    order = lag_order()
    spectra = gather_lag(own_spec)
    spacing = samples // (2 * band_size)
    tap_delays = jnp.arange(LAGS, dtype=jnp.int32) * spacing
    lag_list = jnp.concatenate([tap_delays, gap_samples[0] + tap_delays])
    cosine, sine = wave(lag_list, samples, band_size)
    turn = jnp.where(jnp.arange(2 * LAGS) < LAGS, 1.0, -1.0).astype(f32)[:, None]
    partial_value = correlate(order, own_rows, cosine, turn * sine, spectra)
    channels = partial_value.shape[1]
    total_shots = shot_count * lax.axis_size("shot")
    scale = (1.0 / samples) * (1.0 / (samples * total_shots))
    summed = sum_over_shot(partial_value) * scale
    summed = summed.reshape(2 * LAGS, local_chan, channels)
    correlation = gather_lag(summed[:LAGS])
    filter_bf = solve_filter(order, correlation, summed[LAGS:])
    return inverse(order, filter_bf, spectra, own_rows, cosine[LAGS:], sine[LAGS:], live, waves, samples)


def solution(mesh):
    placed = (P("shot", "lag", None), P("shot", "lag"), P())
    return jax.shard_map(
        shards, mesh=mesh, in_specs=placed, out_specs=P("shot", "lag", None), check_vma=False
    )
```

```python
import jax
import jax.numpy as jnp
from jax import lax
from jax.experimental import pallas as pl
from jax.experimental.pallas import tpu as pltpu
from jax.sharding import PartitionSpec as P

LAGS = 4
CHUNK = 4096
BACK_CHUNK = 4096
FINE = 128
f32 = jnp.float32
bf = jnp.bfloat16
VM = pl.BlockSpec(memory_space=pltpu.VMEM)


def wave(times, samples, band_size):
    harmonic = jnp.arange(1, band_size + 1, dtype=jnp.int32)
    phase = times[:, None] * harmonic[None, :] % (2 * samples)
    angle = phase.astype(f32) * (jnp.pi / samples)
    return jnp.cos(angle), jnp.sin(angle)

def quarter_turn(even, odd, sign):
    turn = (lax.broadcasted_iota(jnp.int32, even.shape, 1) + 1) % 4
    cross = jnp.where(turn == 1, sign, jnp.where(turn == 3, -sign, 0.0)).astype(f32)
    along = jnp.where(turn == 0, 1.0, jnp.where(turn == 2, -1.0, 0.0)).astype(f32)
    return even * along - odd * cross, odd * along + even * cross


def fill_table(step, wave_refs, table_ref):
    cc_ref, cs_ref, fc_ref, fs_ref = wave_refs
    fine, band = fc_ref.shape
    count = table_ref.shape[0] // fine
    for r in range(count):
        cc = cc_ref[pl.ds(step * count + r, 1), :]
        cs = cs_ref[pl.ds(step * count + r, 1), :]
        at = slice(r * fine, (r + 1) * fine)
        table_ref[at, :band] = (cc * fc_ref[...] - cs * fs_ref[...]).astype(bf)
        table_ref[at, band:] = (cs * fc_ref[...] + cc * fs_ref[...]).astype(bf)


def forward_kernel(early_ref, late_ref, live_ref, cc_ref, cs_ref, fc_ref, fs_ref, spec_ref, acc, table_ref):
    step = pl.program_id(0)
    chunk, width = table_ref.shape
    band = width // 2
    rows = spec_ref.shape[0]
    fill_table(step, (cc_ref, cs_ref, fc_ref, fs_ref), table_ref)
    both = jnp.concatenate(
        [early_ref[...].reshape(rows, chunk), late_ref[...].reshape(rows, chunk)], axis=0
    )
    part = jnp.dot(both, table_ref[...], preferred_element_type=f32)

    @pl.when(step == 0)
    def _():
        acc[...] = part

    @pl.when(step > 0)
    def _():
        acc[...] += part

    @pl.when(step == pl.num_programs(0) - 1)
    def _():
        even, odd = quarter_turn(acc[rows:, :band], acc[rows:, band:], 1.0)
        spec_ref[:, :band] = ((acc[:rows, :band] + even) * live_ref[...]).astype(bf)
        spec_ref[:, band:] = ((acc[:rows, band:] + odd) * live_ref[...]).astype(bf)


def forward(traces, live, waves):
    shots, chans, samples = traces.shape
    band = samples // 16
    rows = shots * chans
    steps = samples // 2 // CHUNK
    return pl.pallas_call(
        forward_kernel,
        grid=(steps,),
        out_shape=jax.ShapeDtypeStruct((rows, 2 * band), bf),
        in_specs=[
            pl.BlockSpec((shots, chans, CHUNK), lambda i: (0, 0, i)),
            pl.BlockSpec((shots, chans, CHUNK), lambda i: (0, 0, i + steps)),
        ]
        + [VM] * 5,
        out_specs=pl.BlockSpec((rows, 2 * band), lambda i: (0, 0)),
        scratch_shapes=[pltpu.VMEM((2 * rows, 2 * band), f32), pltpu.VMEM((CHUNK, 2 * band), bf)],
        compiler_params=pltpu.CompilerParams(vmem_limit_bytes=40 * 2**20),
    )(traces, traces, live.reshape(rows, 1), *waves)


def inverse_kernel(order_ref, filter_ref, own_ref, cos_ref, sin_ref, live_ref, *refs):
    wave_refs = refs[:4]
    *piece_refs, out_ref, error, full, later, table_ref = refs[4:]
    half = pl.program_id(1)
    rows = own_ref.shape[0]
    shots, chans, chunk = out_ref.shape
    band = cos_ref.shape[1]

    @pl.when((pl.program_id(0) == 0) & (half == 0))
    def _():
        weights = filter_ref[...].reshape(LAGS * chans, filter_ref.shape[2])
        for s in range(shots):
            place(order_ref, piece_refs, s, full)
            mixed = jnp.dot(weights, full[...], preferred_element_type=f32)
            even = jnp.zeros((chans, band), f32)
            odd = jnp.zeros((chans, band), f32)
            for j in range(LAGS):
                part = mixed[j * chans : (j + 1) * chans]
                c, n = cos_ref[j : j + 1, :], sin_ref[j : j + 1, :]
                even = even + (part[:, :band] * c - part[:, band:] * n)
                odd = odd + (part[:, band:] * c + part[:, :band] * n)
            at = slice(s * chans, (s + 1) * chans)
            error[at, :band] = (own_ref[at, :band].astype(f32) - even).astype(bf)
            error[at, band:] = (own_ref[at, band:].astype(f32) - odd).astype(bf)

        turned = quarter_turn(error[:rows, :band].astype(f32), error[:rows, band:].astype(f32), -1.0)
        error[rows:, :band] = turned[0].astype(bf)
        error[rows:, band:] = turned[1].astype(bf)

    samples = 2 * pl.num_programs(0) * chunk

    @pl.when(half == 0)
    def _():
        fill_table(pl.program_id(0), wave_refs, table_ref)
        restored = lax.dot_general(
            error[...], table_ref[...], (((1,), (1,)), ((), ())), preferred_element_type=f32
        )
        later[...] = (restored[rows:] * (1.0 / samples) * live_ref[...]).astype(bf)
        out_ref[...] = (restored[:rows] * (1.0 / samples) * live_ref[...]).astype(bf).reshape(out_ref.shape)

    @pl.when(half == 1)
    def _():
        out_ref[...] = later[...].reshape(out_ref.shape)


def inverse(order, filter_bf, pieces, own_rows, cosine, sine, live, waves, samples):
    shots, chans = live.shape
    rows, width = own_rows.shape
    steps = samples // 2 // BACK_CHUNK
    channels = filter_bf.shape[2]
    return pl.pallas_call(
        inverse_kernel,
        grid=(steps, 2),
        out_shape=jax.ShapeDtypeStruct((shots, chans, samples), bf),
        in_specs=[pl.BlockSpec(memory_space=pltpu.SMEM)]
        + [VM] * (9 + len(pieces)),
        out_specs=pl.BlockSpec((shots, chans, BACK_CHUNK), lambda i, h: (0, 0, i + h * steps)),
        scratch_shapes=[
            pltpu.VMEM((2 * rows, width), bf),
            pltpu.VMEM((channels, width), bf),
            pltpu.VMEM((rows, BACK_CHUNK), bf),
            pltpu.VMEM((BACK_CHUNK, width), bf),
        ],
        compiler_params=pltpu.CompilerParams(vmem_limit_bytes=40 * 2**20),
    )(order, filter_bf, own_rows, cosine, sine, live.reshape(rows, 1), *waves, *pieces)


def invert_128(groups, spare):
    lane = lax.broadcasted_iota(jnp.int32, (8, 128), 1)
    sub = lax.broadcasted_iota(jnp.int32, (8, 128), 0)
    groups = list(groups)
    for s in range(16):
        lo = 8 * s
        inside = (lane >= lo) & (lane < lo + 8)
        rows = groups[s]
        unit = jnp.where(lane - lo == sub, 1.0, 0.0)
        for j in range(8):
            spare[s % 2, j] = jnp.broadcast_to(rows[:, lo + j : lo + j + 1], (8, 128))
        spare[s % 2, 8] = jnp.where(inside, unit, rows)
        entry = {
            (i, j): jnp.broadcast_to(spare[s % 2, j, i : i + 1, :], (8, 128))
            for j in range(8)
            for i in range(j, 8)
        }
        y = [jnp.broadcast_to(spare[s % 2, 8, j : j + 1, :], (8, 128)) for j in range(8)]
        low = {}
        dinv = []
        for j in range(8):
            d = 1.0 / entry[j, j]
            dinv.append(d)
            for i in range(j + 1, 8):
                low[i, j] = entry[i, j] * d
            for i in range(j + 1, 8):
                for k in range(j + 1, i + 1):
                    entry[i, k] = entry[i, k] - low[i, j] * entry[k, j]
                y[i] = y[i] - low[i, j] * y[j]
        v = [None] * 8
        for j in reversed(range(8)):
            t = y[j] * dinv[j]
            for i in range(j + 1, 8):
                t = t - low[i, j] * v[i]
            v[j] = t
        order = [(s + 1 + g) % 16 for g in range(15)]
        for g in order:
            x = groups[g]
            t = jnp.where(inside, 0.0, x)
            for j in range(8):
                t = t - jnp.broadcast_to(x[:, lo+j:lo+j+1], (8, 128)) * v[j]
            groups[g] = t
        t = v[0]
        for j in range(1, 8):
            t = jnp.where(sub == j, v[j], t)
        groups[s] = t
    return groups


def mm(a, b, ca=1, cb=0):
    return lax.dot_general(a, b, (((ca,), (cb,)), ((), ())), precision=lax.Precision.HIGHEST, preferred_element_type=f32)

def solve_kernel(order_ref, rhs_ref, *refs):
    *piece_refs, out_ref, columns, gains, block, whole, spare = refs
    chans, n = rhs_ref.shape[1:]
    h = n // 2
    end = LAGS * n + chans
    count = 0
    for ref in piece_refs:
        for i in range(ref.shape[0]):
            start = pl.multiple_of(order_ref[count] * chans, chans)
            for k in range(LAGS):
                for j in range(LAGS - k):
                    columns[j, pl.ds((j + k) * n + start, chans), :] = ref[i, k]
            count += 1
    for j in range(LAGS):
        columns[j, LAGS * n :, :] = rhs_ref[j]
    row = lax.broadcasted_iota(jnp.int32, (n, n), 0)
    eye = row == lax.broadcasted_iota(jnp.int32, (n, n), 1)
    whiten = 0.1 * jnp.sum(jnp.where(eye, columns[0, :n], 0.0)) / n + 1e-06
    whiten = jnp.where(eye[:h, :h], whiten, 0.0)
    block[...] = columns[0, :h, :h] + whiten

    def first_half(p):
        inv = block[...]
        corner = columns[p, p * n + h : (p + 1) * n, :h]
        left = mm(corner, inv)
        whole[:h, :h] = inv
        whole[h:, :h] = left
        block[...] = columns[p, p * n + h : (p + 1) * n, h:] + whiten - mm(left, corner, 1, 1)

    def second_half(p):
        inv = block[...]
        left = whole[h:, :h]
        low = mm(inv, left)
        whole[:h, :h] += mm(left, low, 0, 0)
        whole[h:, :h] = -low
        whole[:h, h:] = -low.T
        whole[h:, h:] = inv
        below = (p + 1) * n
        gain = mm(columns[p, below:, :], whole[...])
        gains[p, below:, :] = gain
        for j in range(p + 1, LAGS):
            columns[j, j * n :, :] -= mm(gain[j * n - below :], columns[p, j * n : (j + 1) * n, :], 1, 1)
        if p + 1 < LAGS:
            block[...] = columns[p + 1, below : below + h, :h] + whiten

    def step(q, carry):
        even = 0.5 * (block[...] + block[...].T)
        groups = invert_128([even[8 * i : 8 * i + 8, :] for i in range(16)], spare)
        for i in range(16):
            block[8 * i : 8 * i + 8, :] = groups[i]
        for p in range(LAGS):
            pl.when(q == 2 * p)(lambda p=p: first_half(p))
            pl.when(q == 2 * p + 1)(lambda p=p: second_half(p))
        return carry

    lax.fori_loop(0, 2 * LAGS, step, 0)
    solved = {}
    for p in reversed(range(LAGS)):
        x = gains[p, LAGS * n : end, :]
        for j in range(p + 1, LAGS):
            x = x - mm(solved[j], gains[p, j * n : (j + 1) * n, :])
        solved[p] = x
        out_ref[p] = x.astype(out_ref.dtype)


def solve_filter(order, pieces, rhs):
    chans = rhs.shape[1]
    n = rhs.shape[2]
    half = n // 2
    return pl.pallas_call(
        solve_kernel,
        out_shape=jax.ShapeDtypeStruct((LAGS, chans, n), bf),
        in_specs=[pl.BlockSpec(memory_space=pltpu.SMEM)] + [VM] * (1 + len(pieces)),
        out_specs=VM,
        scratch_shapes=[
            pltpu.VMEM((LAGS, LAGS * n + chans, n), f32),
            pltpu.VMEM((LAGS, LAGS * n + chans, n), f32),
            pltpu.VMEM((half, half), f32),
            pltpu.VMEM((n, n), f32),
            pltpu.VMEM((2, 9, 8, half), f32),
        ],
        compiler_params=pltpu.CompilerParams(vmem_limit_bytes=40 * 2**20),
    )(order, rhs, *pieces)


def place(order_ref, piece_refs, shot, full):
    count = 0
    for ref in piece_refs:
        for i in range(ref.shape[0]):
            rows = ref.shape[2]
            full[pl.ds(pl.multiple_of(order_ref[count] * rows, rows), rows), :] = ref[i, shot]
            count += 1


def correlate_kernel(order_ref, own_ref, cos_ref, sin_ref, *refs):
    *piece_refs, out_ref, rotated, full = refs
    shots = piece_refs[0].shape[1]
    chans = piece_refs[0].shape[2]
    band = cos_ref.shape[1]
    for s in range(shots):
        place(order_ref, piece_refs, s, full)
        even = own_ref[s * chans : (s + 1) * chans, :band].astype(f32)
        odd = own_ref[s * chans : (s + 1) * chans, band:].astype(f32)
        for k in range(2 * LAGS):
            c, n = cos_ref[k : k + 1, :], sin_ref[k : k + 1, :]
            at = slice(k * chans, (k + 1) * chans)
            rotated[at, :band] = (even * c - odd * n).astype(bf)
            rotated[at, band:] = (odd * c + even * n).astype(bf)
        part = lax.dot_general(
            rotated[...], full[...], (((1,), (1,)), ((), ())), preferred_element_type=f32
        )
        if s == 0:
            out_ref[...] = part
        else:
            out_ref[...] += part


def correlate(order, own_rows, cosine, sine, pieces):
    width = own_rows.shape[1]
    chans = pieces[0].shape[2]
    channels = chans * order.shape[0]
    rows = 2 * LAGS * chans
    return pl.pallas_call(
        correlate_kernel,
        out_shape=jax.ShapeDtypeStruct((rows, channels), f32),
        in_specs=[pl.BlockSpec(memory_space=pltpu.SMEM)] + [VM] * (3 + len(pieces)),
        out_specs=VM,
        scratch_shapes=[pltpu.VMEM((rows, width), bf), pltpu.VMEM((channels, width), bf)],
        compiler_params=pltpu.CompilerParams(vmem_limit_bytes=40 * 2**20),
    )(order, own_rows, cosine, sine, *pieces)


def lag_moves():
    def move(dx, dy, dc):
        return [
            ((x * 4 + y) * 2 + c, ((x ^ dx) * 4 + (y + dy) % 4) * 2 + (c ^ dc))
            for x in range(2)
            for y in range(4)
            for c in range(2)
        ]

    return move(1, 0, 0), move(0, 1, 0), move(0, -1, 0), move(0, 0, 1)


def gather_lag(value):
    over_x, up, down, over_core = lag_moves()
    own = value[None]
    pair = jnp.concatenate([own, lax.ppermute(own, "lag", over_x)], axis=0)
    below = lax.ppermute(pair, "lag", up)
    above = lax.ppermute(pair, "lag", down)
    far_own = lax.ppermute(below[:1], "lag", up)
    far_other = lax.ppermute(above[1:], "lag", down)
    near = [pair, below, above, far_own, far_other]
    return near + [lax.ppermute(piece, "lag", over_core) for piece in near]


def lag_order():
    index = lax.axis_index("lag")
    x, y, core = index // 8, index // 2 % 4, index % 2
    places = [
        (x ^ dx) * 8 + (y + dy) % 4 * 2 + (core ^ dc)
        for dc in (0, 1)
        for dx, dy in ((0, 0), (1, 0), (0, 3), (1, 3), (0, 1), (1, 1), (0, 2), (1, 2))
    ]
    return jnp.stack(places).astype(jnp.int32)


def sum_over_shot(value):
    half = value.shape[0] // 2
    odd = lax.axis_index("shot") % 2 == 1

    def other(part, bit):
        return lax.ppermute(part, "shot", [(i, i ^ bit) for i in range(16)])

    first, second = value[:half], value[half:]
    held = jnp.where(odd, second, first) + other(jnp.where(odd, first, second), 1)
    for bit in (2, 4, 8):
        held = held + other(held, bit)
    back = other(held, 1)
    return jnp.where(odd, back, held), jnp.where(odd, held, back)


def shards(traces, live_mask, gap_samples):
    shot_count, local_chan, samples = traces.shape
    band_size = samples // 16
    live = live_mask.astype(f32)
    coarse = jnp.arange(samples // 2 // FINE, dtype=jnp.int32) * FINE
    waves = wave(coarse, samples, band_size) + wave(jnp.arange(FINE, dtype=jnp.int32), samples, band_size)
    own_rows = forward(traces, live, waves)
    own_spec = own_rows.reshape(shot_count, local_chan, 2 * band_size)
    order = lag_order()
    spectra = gather_lag(own_spec)
    spacing = samples // (2 * band_size)
    tap_delays = jnp.arange(LAGS, dtype=jnp.int32) * spacing
    lag_list = jnp.concatenate([tap_delays, gap_samples[0] + tap_delays])
    cosine, sine = wave(lag_list, samples, band_size)
    turn = jnp.where(jnp.arange(2 * LAGS) < LAGS, 1.0, -1.0).astype(f32)[:, None]
    partial_value = correlate(order, own_rows, cosine, turn * sine, spectra)
    channels = partial_value.shape[1]
    total_shots = shot_count * lax.axis_size("shot")
    scale = (1.0 / samples) * (1.0 / (samples * total_shots))
    shape = (LAGS, local_chan, channels)
    system, targets = sum_over_shot(partial_value)
    correlation = gather_lag((system * scale).reshape(shape))
    filter_bf = solve_filter(order, correlation, (targets * scale).reshape(shape))
    return inverse(order, filter_bf, spectra, own_rows, cosine[LAGS:], sine[LAGS:], live, waves, samples)


def solution(mesh):
    placed = (P("shot", "lag", None), P("shot", "lag"), P())
    return jax.shard_map(
        shards, mesh=mesh, in_specs=placed, out_specs=P("shot", "lag", None), check_vma=False
    )
```

```python
import jax
import jax.numpy as jnp
from jax import lax
from jax.experimental import pallas as pl
from jax.experimental.pallas import tpu as pltpu
from jax.sharding import PartitionSpec as P

LAGS = 4
CHUNK = 4096
BACK_CHUNK = 4096
FINE = 128
f32 = jnp.float32
bf = jnp.bfloat16
VM = pl.BlockSpec(memory_space=pltpu.VMEM)


def wave(times, samples, band_size):
    harmonic = jnp.arange(1, band_size + 1, dtype=jnp.int32)
    phase = times[:, None] * harmonic[None, :] % (2 * samples)
    angle = phase.astype(f32) * (jnp.pi / samples)
    return jnp.cos(angle), jnp.sin(angle)

def quarter_turn(even, odd, sign):
    turn = (lax.broadcasted_iota(jnp.int32, even.shape, 1) + 1) % 4
    cross = jnp.where(turn == 1, sign, jnp.where(turn == 3, -sign, 0.0)).astype(f32)
    along = jnp.where(turn == 0, 1.0, jnp.where(turn == 2, -1.0, 0.0)).astype(f32)
    return even * along - odd * cross, odd * along + even * cross


def fill_table(step, wave_refs, table_ref):
    cc_ref, cs_ref, fc_ref, fs_ref = wave_refs
    fine, band = fc_ref.shape
    count = table_ref.shape[0] // fine
    for r in range(count):
        cc = cc_ref[pl.ds(step * count + r, 1), :]
        cs = cs_ref[pl.ds(step * count + r, 1), :]
        at = slice(r * fine, (r + 1) * fine)
        table_ref[at, :band] = (cc * fc_ref[...] - cs * fs_ref[...]).astype(bf)
        table_ref[at, band:] = (cs * fc_ref[...] + cc * fs_ref[...]).astype(bf)


def forward_kernel(early_ref, late_ref, live_ref, cc_ref, cs_ref, fc_ref, fs_ref, spec_ref, acc, table_ref):
    step = pl.program_id(0)
    chunk, width = table_ref.shape
    band = width // 2
    rows = spec_ref.shape[0]
    fill_table(step, (cc_ref, cs_ref, fc_ref, fs_ref), table_ref)
    both = jnp.concatenate(
        [early_ref[...].reshape(rows, chunk), late_ref[...].reshape(rows, chunk)], axis=0
    )
    part = jnp.dot(both, table_ref[...], preferred_element_type=f32)

    @pl.when(step == 0)
    def _():
        acc[...] = part

    @pl.when(step > 0)
    def _():
        acc[...] += part

    @pl.when(step == pl.num_programs(0) - 1)
    def _():
        even, odd = quarter_turn(acc[rows:, :band], acc[rows:, band:], 1.0)
        spec_ref[:, :band] = ((acc[:rows, :band] + even) * live_ref[...]).astype(bf)
        spec_ref[:, band:] = ((acc[:rows, band:] + odd) * live_ref[...]).astype(bf)


def forward(traces, live, waves):
    shots, chans, samples = traces.shape
    band = samples // 16
    rows = shots * chans
    steps = samples // 2 // CHUNK
    return pl.pallas_call(
        forward_kernel,
        grid=(steps,),
        out_shape=jax.ShapeDtypeStruct((rows, 2 * band), bf),
        in_specs=[
            pl.BlockSpec((shots, chans, CHUNK), lambda i: (0, 0, i)),
            pl.BlockSpec((shots, chans, CHUNK), lambda i: (0, 0, i + steps)),
        ]
        + [VM] * 5,
        out_specs=pl.BlockSpec((rows, 2 * band), lambda i: (0, 0)),
        scratch_shapes=[pltpu.VMEM((2 * rows, 2 * band), f32), pltpu.VMEM((CHUNK, 2 * band), bf)],
        compiler_params=pltpu.CompilerParams(vmem_limit_bytes=40 * 2**20),
    )(traces, traces, live.reshape(rows, 1), *waves)


def inverse_kernel(order_ref, filter_ref, own_ref, cos_ref, sin_ref, live_ref, *refs):
    wave_refs = refs[:4]
    *piece_refs, out_ref, error, full, later, table_ref = refs[4:]
    half = pl.program_id(1)
    rows = own_ref.shape[0]
    shots, chans, chunk = out_ref.shape
    band = cos_ref.shape[1]

    @pl.when((pl.program_id(0) == 0) & (half == 0))
    def _():
        weights = filter_ref[...].reshape(LAGS * chans, filter_ref.shape[2])
        for s in range(shots):
            place(order_ref, piece_refs, s, full)
            mixed = jnp.dot(weights, full[...], preferred_element_type=f32)
            even = jnp.zeros((chans, band), f32)
            odd = jnp.zeros((chans, band), f32)
            for j in range(LAGS):
                part = mixed[j * chans : (j + 1) * chans]
                c, n = cos_ref[j : j + 1, :], sin_ref[j : j + 1, :]
                even = even + (part[:, :band] * c - part[:, band:] * n)
                odd = odd + (part[:, band:] * c + part[:, :band] * n)
            at = slice(s * chans, (s + 1) * chans)
            error[at, :band] = (own_ref[at, :band].astype(f32) - even).astype(bf)
            error[at, band:] = (own_ref[at, band:].astype(f32) - odd).astype(bf)

        turned = quarter_turn(error[:rows, :band].astype(f32), error[:rows, band:].astype(f32), -1.0)
        error[rows:, :band] = turned[0].astype(bf)
        error[rows:, band:] = turned[1].astype(bf)

    samples = 2 * pl.num_programs(0) * chunk

    @pl.when(half == 0)
    def _():
        fill_table(pl.program_id(0), wave_refs, table_ref)
        restored = lax.dot_general(
            error[...], table_ref[...], (((1,), (1,)), ((), ())), preferred_element_type=f32
        )
        later[...] = (restored[rows:] * (1.0 / samples) * live_ref[...]).astype(bf)
        out_ref[...] = (restored[:rows] * (1.0 / samples) * live_ref[...]).astype(bf).reshape(out_ref.shape)

    @pl.when(half == 1)
    def _():
        out_ref[...] = later[...].reshape(out_ref.shape)


def inverse(order, filter_bf, pieces, own_rows, cosine, sine, live, waves, samples):
    shots, chans = live.shape
    rows, width = own_rows.shape
    steps = samples // 2 // BACK_CHUNK
    channels = filter_bf.shape[2]
    return pl.pallas_call(
        inverse_kernel,
        grid=(steps, 2),
        out_shape=jax.ShapeDtypeStruct((shots, chans, samples), bf),
        in_specs=[pl.BlockSpec(memory_space=pltpu.SMEM)]
        + [VM] * (9 + len(pieces)),
        out_specs=pl.BlockSpec((shots, chans, BACK_CHUNK), lambda i, h: (0, 0, i + h * steps)),
        scratch_shapes=[
            pltpu.VMEM((2 * rows, width), bf),
            pltpu.VMEM((channels, width), bf),
            pltpu.VMEM((rows, BACK_CHUNK), bf),
            pltpu.VMEM((BACK_CHUNK, width), bf),
        ],
        compiler_params=pltpu.CompilerParams(vmem_limit_bytes=40 * 2**20),
    )(order, filter_bf, own_rows, cosine, sine, live.reshape(rows, 1), *waves, *pieces)


def invert_128(groups, spare):
    lane = lax.broadcasted_iota(jnp.int32, (8, 128), 1)
    sub = lax.broadcasted_iota(jnp.int32, (8, 128), 0)
    groups = list(groups)
    for s in range(16):
        lo = 8 * s
        inside = (lane >= lo) & (lane < lo + 8)
        rows = groups[s]
        unit = jnp.where(lane - lo == sub, 1.0, 0.0)
        for j in range(8):
            spare[s % 2, j] = jnp.broadcast_to(rows[:, lo + j : lo + j + 1], (8, 128))
        spare[s % 2, 8] = jnp.where(inside, unit, rows)
        entry = {
            (i, j): jnp.broadcast_to(spare[s % 2, j, i : i + 1, :], (8, 128))
            for j in range(8)
            for i in range(j, 8)
        }
        y = [jnp.broadcast_to(spare[s % 2, 8, j : j + 1, :], (8, 128)) for j in range(8)]
        low = {}
        dinv = []
        for j in range(8):
            d = 1.0 / entry[j, j]
            dinv.append(d)
            for i in range(j + 1, 8):
                low[i, j] = entry[i, j] * d
            for i in range(j + 1, 8):
                for k in range(j + 1, i + 1):
                    entry[i, k] = entry[i, k] - low[i, j] * entry[k, j]
                y[i] = y[i] - low[i, j] * y[j]
        v = [None] * 8
        for j in reversed(range(8)):
            t = y[j] * dinv[j]
            for i in range(j + 1, 8):
                t = t - low[i, j] * v[i]
            v[j] = t
        order = [(s + 1 + g) % 16 for g in range(15)]
        for g in order:
            x = groups[g]
            t = jnp.where(inside, 0.0, x)
            for j in range(8):
                t = t - jnp.broadcast_to(x[:, lo+j:lo+j+1], (8, 128)) * v[j]
            groups[g] = t
        t = v[0]
        for j in range(1, 8):
            t = jnp.where(sub == j, v[j], t)
        groups[s] = t
    return groups


def mm(a, b, ca=1, cb=0):
    return lax.dot_general(a, b, (((ca,), (cb,)), ((), ())), precision=lax.Precision.HIGHEST, preferred_element_type=f32)

def solve_kernel(order_ref, rhs_ref, *refs):
    *piece_refs, out_ref, columns, gains, block, whole, spare = refs
    chans, n = rhs_ref.shape[1:]
    h = n // 2
    end = LAGS * n + chans
    count = 0
    for ref in piece_refs:
        for i in range(ref.shape[0]):
            start = pl.multiple_of(order_ref[count] * chans, chans)
            for k in range(LAGS):
                for j in range(LAGS - k):
                    columns[j, pl.ds((j + k) * n + start, chans), :] = ref[i, k]
            count += 1
    for j in range(LAGS):
        columns[j, LAGS * n :, :] = rhs_ref[j]
    row = lax.broadcasted_iota(jnp.int32, (n, n), 0)
    eye = row == lax.broadcasted_iota(jnp.int32, (n, n), 1)
    whiten = 0.1 * jnp.sum(jnp.where(eye, columns[0, :n], 0.0)) / n + 1e-06
    whiten = jnp.where(eye[:h, :h], whiten, 0.0)
    block[...] = columns[0, :h, :h] + whiten

    def first_half(p):
        inv = block[...]
        corner = columns[p, p * n + h : (p + 1) * n, :h]
        left = mm(corner, inv)
        whole[:h, :h] = inv
        whole[h:, :h] = left
        block[...] = columns[p, p * n + h : (p + 1) * n, h:] + whiten - mm(left, corner, 1, 1)

    def second_half(p):
        inv = block[...]
        left = whole[h:, :h]
        low = mm(inv, left)
        whole[:h, :h] += mm(left, low, 0, 0)
        whole[h:, :h] = -low
        whole[:h, h:] = -low.T
        whole[h:, h:] = inv
        below = (p + 1) * n
        gain = mm(columns[p, below:, :], whole[...])
        gains[p, below:, :] = gain
        for j in range(p + 1, LAGS):
            columns[j, j * n :, :] -= mm(gain[j * n - below :], columns[p, j * n : (j + 1) * n, :], 1, 1)
        if p + 1 < LAGS:
            block[...] = columns[p + 1, below : below + h, :h] + whiten

    def step(q, carry):
        even = 0.5 * (block[...] + block[...].T)
        groups = invert_128([even[8 * i : 8 * i + 8, :] for i in range(16)], spare)
        for i in range(16):
            block[8 * i : 8 * i + 8, :] = groups[i]
        for p in range(LAGS):
            pl.when(q == 2 * p)(lambda p=p: first_half(p))
            pl.when(q == 2 * p + 1)(lambda p=p: second_half(p))
        return carry

    lax.fori_loop(0, 2 * LAGS, step, 0)
    solved = {}
    for p in reversed(range(LAGS)):
        x = gains[p, LAGS * n : end, :]
        for j in range(p + 1, LAGS):
            x = x - mm(solved[j], gains[p, j * n : (j + 1) * n, :])
        solved[p] = x
        out_ref[p] = x.astype(out_ref.dtype)


def solve_filter(order, pieces, rhs):
    chans = rhs.shape[1]
    n = rhs.shape[2]
    half = n // 2
    return pl.pallas_call(
        solve_kernel,
        out_shape=jax.ShapeDtypeStruct((LAGS, chans, n), bf),
        in_specs=[pl.BlockSpec(memory_space=pltpu.SMEM)] + [VM] * (1 + len(pieces)),
        out_specs=VM,
        scratch_shapes=[
            pltpu.VMEM((LAGS, LAGS * n + chans, n), f32),
            pltpu.VMEM((LAGS, LAGS * n + chans, n), f32),
            pltpu.VMEM((half, half), f32),
            pltpu.VMEM((n, n), f32),
            pltpu.VMEM((2, 9, 8, half), f32),
        ],
        compiler_params=pltpu.CompilerParams(vmem_limit_bytes=40 * 2**20),
    )(order, rhs, *pieces)


def place(order_ref, piece_refs, shot, full):
    count = 0
    for ref in piece_refs:
        for i in range(ref.shape[0]):
            rows = ref.shape[2]
            full[pl.ds(pl.multiple_of(order_ref[count] * rows, rows), rows), :] = ref[i, shot]
            count += 1


def correlate_kernel(order_ref, own_ref, cos_ref, sin_ref, *refs):
    *piece_refs, out_ref, rotated, full = refs
    shots = piece_refs[0].shape[1]
    chans = piece_refs[0].shape[2]
    band = cos_ref.shape[1]
    for s in range(shots):
        place(order_ref, piece_refs, s, full)
        even = own_ref[s * chans : (s + 1) * chans, :band].astype(f32)
        odd = own_ref[s * chans : (s + 1) * chans, band:].astype(f32)
        for k in range(2 * LAGS):
            c, n = cos_ref[k : k + 1, :], sin_ref[k : k + 1, :]
            at = slice(k * chans, (k + 1) * chans)
            rotated[at, :band] = (even * c - odd * n).astype(bf)
            rotated[at, band:] = (odd * c + even * n).astype(bf)
        part = lax.dot_general(
            rotated[...], full[...], (((1,), (1,)), ((), ())), preferred_element_type=f32
        )
        if s == 0:
            out_ref[...] = part
        else:
            out_ref[...] += part


def correlate(order, own_rows, cosine, sine, pieces):
    width = own_rows.shape[1]
    chans = pieces[0].shape[2]
    channels = chans * order.shape[0]
    rows = 2 * LAGS * chans
    return pl.pallas_call(
        correlate_kernel,
        out_shape=jax.ShapeDtypeStruct((rows, channels), f32),
        in_specs=[pl.BlockSpec(memory_space=pltpu.SMEM)] + [VM] * (3 + len(pieces)),
        out_specs=VM,
        scratch_shapes=[pltpu.VMEM((rows, width), bf), pltpu.VMEM((channels, width), bf)],
        compiler_params=pltpu.CompilerParams(vmem_limit_bytes=40 * 2**20),
    )(order, own_rows, cosine, sine, *pieces)


def lag_moves():
    def move(dx, dy, dc):
        return [
            ((x * 4 + y) * 2 + c, ((x ^ dx) * 4 + (y + dy) % 4) * 2 + (c ^ dc))
            for x in range(2)
            for y in range(4)
            for c in range(2)
        ]

    return move(1, 0, 0), move(0, 1, 0), move(0, -1, 0), move(0, 0, 1)


def gather_lag(value):
    over_x, up, down, over_core = lag_moves()
    own = value[None]
    pair = jnp.concatenate([own, lax.ppermute(own, "lag", over_x)], axis=0)
    below = lax.ppermute(pair, "lag", up)
    above = lax.ppermute(pair, "lag", down)
    far_own = lax.ppermute(below[:1], "lag", up)
    far_other = lax.ppermute(above[1:], "lag", down)
    near = [pair, below, above, far_own, far_other]
    return near + [lax.ppermute(piece, "lag", over_core) for piece in near]


def gather_lag_wide(value):
    over_x, up, down, over_core = lag_moves()
    own = value[None]
    other = lax.ppermute(own, "lag", over_x)
    below_own = lax.ppermute(own, "lag", up)
    above_own = lax.ppermute(own, "lag", down)
    below_other = lax.ppermute(other, "lag", up)
    above_other = lax.ppermute(other, "lag", down)
    far_own = lax.ppermute(below_own, "lag", up)
    far_other = lax.ppermute(above_other, "lag", down)
    near = [own, other, below_own, below_other, above_own, above_other, far_own, far_other]
    return near + [lax.ppermute(piece, "lag", over_core) for piece in near]


def lag_order():
    index = lax.axis_index("lag")
    x, y, core = index // 8, index // 2 % 4, index % 2
    places = [
        (x ^ dx) * 8 + (y + dy) % 4 * 2 + (core ^ dc)
        for dc in (0, 1)
        for dx, dy in ((0, 0), (1, 0), (0, 3), (1, 3), (0, 1), (1, 1), (0, 2), (1, 2))
    ]
    return jnp.stack(places).astype(jnp.int32)


def sum_over_shot(value):
    half = value.shape[0] // 2
    odd = lax.axis_index("shot") % 2 == 1

    def other(part, bit):
        return lax.ppermute(part, "shot", [(i, i ^ bit) for i in range(16)])

    first, second = value[:half], value[half:]
    held = jnp.where(odd, second, first) + other(jnp.where(odd, first, second), 1)
    for bit in (2, 4, 8):
        held = held + other(held, bit)
    back = other(held, 1)
    return jnp.where(odd, back, held), jnp.where(odd, held, back)


def shards(traces, live_mask, gap_samples):
    shot_count, local_chan, samples = traces.shape
    band_size = samples // 16
    live = live_mask.astype(f32)
    coarse = jnp.arange(samples // 2 // FINE, dtype=jnp.int32) * FINE
    waves = wave(coarse, samples, band_size) + wave(jnp.arange(FINE, dtype=jnp.int32), samples, band_size)
    own_rows = forward(traces, live, waves)
    own_spec = own_rows.reshape(shot_count, local_chan, 2 * band_size)
    order = lag_order()
    spectra = gather_lag_wide(own_spec)
    spacing = samples // (2 * band_size)
    tap_delays = jnp.arange(LAGS, dtype=jnp.int32) * spacing
    lag_list = jnp.concatenate([tap_delays, gap_samples[0] + tap_delays])
    cosine, sine = wave(lag_list, samples, band_size)
    turn = jnp.where(jnp.arange(2 * LAGS) < LAGS, 1.0, -1.0).astype(f32)[:, None]
    partial_value = correlate(order, own_rows, cosine, turn * sine, spectra)
    channels = partial_value.shape[1]
    total_shots = shot_count * lax.axis_size("shot")
    scale = (1.0 / samples) * (1.0 / (samples * total_shots))
    shape = (LAGS, local_chan, channels)
    system, targets = sum_over_shot(partial_value)
    correlation = gather_lag((system * scale).reshape(shape))
    filter_bf = solve_filter(order, correlation, (targets * scale).reshape(shape))
    return inverse(order, filter_bf, spectra, own_rows, cosine[LAGS:], sine[LAGS:], live, waves, samples)


def solution(mesh):
    placed = (P("shot", "lag", None), P("shot", "lag"), P())
    return jax.shard_map(
        shards, mesh=mesh, in_specs=placed, out_specs=P("shot", "lag", None), check_vma=False
    )
```

```python
import jax
import jax.numpy as jnp
from jax import lax
from jax.experimental import pallas as pl
from jax.experimental.pallas import tpu as pltpu
from jax.sharding import PartitionSpec as P

LAGS = 4
CHUNK = 4096
BACK_CHUNK = 4096
FINE = 64
f32 = jnp.float32
bf = jnp.bfloat16
VM = pl.BlockSpec(memory_space=pltpu.VMEM)


def wave(times, samples, band_size):
    harmonic = jnp.arange(1, band_size + 1, dtype=jnp.int32)
    phase = times[:, None] * harmonic[None, :] % (2 * samples)
    angle = phase.astype(f32) * (jnp.pi / samples)
    return jnp.cos(angle), jnp.sin(angle)

def quarter_turn(even, odd, sign):
    turn = (lax.broadcasted_iota(jnp.int32, even.shape, 1) + 1) % 4
    cross = jnp.where(turn == 1, sign, jnp.where(turn == 3, -sign, 0.0)).astype(f32)
    along = jnp.where(turn == 0, 1.0, jnp.where(turn == 2, -1.0, 0.0)).astype(f32)
    return even * along - odd * cross, odd * along + even * cross


def fill_table(step, wave_refs, table_ref):
    cc_ref, cs_ref, fc_ref, fs_ref = wave_refs
    fine, band = fc_ref.shape
    count = table_ref.shape[0] // fine
    for r in range(count):
        cc = cc_ref[pl.ds(step * count + r, 1), :]
        cs = cs_ref[pl.ds(step * count + r, 1), :]
        at = slice(r * fine, (r + 1) * fine)
        table_ref[at, :band] = (cc * fc_ref[...] - cs * fs_ref[...]).astype(bf)
        table_ref[at, band:] = (cs * fc_ref[...] + cc * fs_ref[...]).astype(bf)


def forward_kernel(early_ref, late_ref, live_ref, cc_ref, cs_ref, fc_ref, fs_ref, spec_ref, acc, table_ref):
    step = pl.program_id(0)
    chunk, width = table_ref.shape
    band = width // 2
    rows = spec_ref.shape[0]
    fill_table(step, (cc_ref, cs_ref, fc_ref, fs_ref), table_ref)
    both = jnp.concatenate(
        [early_ref[...].reshape(rows, chunk), late_ref[...].reshape(rows, chunk)], axis=0
    )
    part = jnp.dot(both, table_ref[...], preferred_element_type=f32)

    @pl.when(step == 0)
    def _():
        acc[...] = part

    @pl.when(step > 0)
    def _():
        acc[...] += part

    @pl.when(step == pl.num_programs(0) - 1)
    def _():
        even, odd = quarter_turn(acc[rows:, :band], acc[rows:, band:], 1.0)
        spec_ref[:, :band] = ((acc[:rows, :band] + even) * live_ref[...]).astype(bf)
        spec_ref[:, band:] = ((acc[:rows, band:] + odd) * live_ref[...]).astype(bf)


def forward(traces, live, waves):
    shots, chans, samples = traces.shape
    band = samples // 16
    rows = shots * chans
    steps = samples // 2 // CHUNK
    return pl.pallas_call(
        forward_kernel,
        grid=(steps,),
        out_shape=jax.ShapeDtypeStruct((rows, 2 * band), bf),
        in_specs=[
            pl.BlockSpec((shots, chans, CHUNK), lambda i: (0, 0, i)),
            pl.BlockSpec((shots, chans, CHUNK), lambda i: (0, 0, i + steps)),
        ]
        + [VM] * 5,
        out_specs=pl.BlockSpec((rows, 2 * band), lambda i: (0, 0)),
        scratch_shapes=[pltpu.VMEM((2 * rows, 2 * band), f32), pltpu.VMEM((CHUNK, 2 * band), bf)],
        compiler_params=pltpu.CompilerParams(vmem_limit_bytes=60 * 2**20),
    )(traces, traces, live.reshape(rows, 1), *waves)


def inverse_kernel(order_ref, filter_ref, own_ref, cos_ref, sin_ref, live_ref, *refs):
    wave_refs = refs[:4]
    *piece_refs, out_ref, error, full, later, table_ref = refs[4:]
    half = pl.program_id(1)
    rows = own_ref.shape[0]
    shots, chans, chunk = out_ref.shape
    band = cos_ref.shape[1]

    @pl.when((pl.program_id(0) == 0) & (half == 0))
    def _():
        weights = filter_ref[...].reshape(LAGS * chans, filter_ref.shape[2])
        for s in range(shots):
            place(order_ref, piece_refs, s, full)
            mixed = jnp.dot(weights, full[...], preferred_element_type=f32)
            even = jnp.zeros((chans, band), f32)
            odd = jnp.zeros((chans, band), f32)
            for j in range(LAGS):
                part = mixed[j * chans : (j + 1) * chans]
                c, n = cos_ref[j : j + 1, :], sin_ref[j : j + 1, :]
                even = even + (part[:, :band] * c - part[:, band:] * n)
                odd = odd + (part[:, band:] * c + part[:, :band] * n)
            at = slice(s * chans, (s + 1) * chans)
            error[at, :band] = (own_ref[at, :band].astype(f32) - even).astype(bf)
            error[at, band:] = (own_ref[at, band:].astype(f32) - odd).astype(bf)

        turned = quarter_turn(error[:rows, :band].astype(f32), error[:rows, band:].astype(f32), -1.0)
        error[rows:, :band] = turned[0].astype(bf)
        error[rows:, band:] = turned[1].astype(bf)

    samples = 2 * pl.num_programs(0) * chunk

    @pl.when(half == 0)
    def _():
        fill_table(pl.program_id(0), wave_refs, table_ref)
        restored = lax.dot_general(
            error[...], table_ref[...], (((1,), (1,)), ((), ())), preferred_element_type=f32
        )
        later[...] = (restored[rows:] * (1.0 / samples) * live_ref[...]).astype(bf)
        out_ref[...] = (restored[:rows] * (1.0 / samples) * live_ref[...]).astype(bf).reshape(out_ref.shape)

    @pl.when(half == 1)
    def _():
        out_ref[...] = later[...].reshape(out_ref.shape)


def inverse(order, filter_bf, pieces, own_rows, cosine, sine, live, waves, samples):
    shots, chans = live.shape
    rows, width = own_rows.shape
    steps = samples // 2 // BACK_CHUNK
    channels = filter_bf.shape[2]
    return pl.pallas_call(
        inverse_kernel,
        grid=(steps, 2),
        out_shape=jax.ShapeDtypeStruct((shots, chans, samples), bf),
        in_specs=[pl.BlockSpec(memory_space=pltpu.SMEM)]
        + [VM] * (9 + len(pieces)),
        out_specs=pl.BlockSpec((shots, chans, BACK_CHUNK), lambda i, h: (0, 0, i + h * steps)),
        scratch_shapes=[
            pltpu.VMEM((2 * rows, width), bf),
            pltpu.VMEM((channels, width), bf),
            pltpu.VMEM((rows, BACK_CHUNK), bf),
            pltpu.VMEM((BACK_CHUNK, width), bf),
        ],
        compiler_params=pltpu.CompilerParams(vmem_limit_bytes=40 * 2**20),
    )(order, filter_bf, own_rows, cosine, sine, live.reshape(rows, 1), *waves, *pieces)


def invert_128(groups, spare):
    lane = lax.broadcasted_iota(jnp.int32, (8, 128), 1)
    sub = lax.broadcasted_iota(jnp.int32, (8, 128), 0)
    groups = list(groups)
    for s in range(16):
        lo = 8 * s
        inside = (lane >= lo) & (lane < lo + 8)
        rows = groups[s]
        unit = jnp.where(lane - lo == sub, 1.0, 0.0)
        for j in range(8):
            spare[s % 2, j] = jnp.broadcast_to(rows[:, lo + j : lo + j + 1], (8, 128))
        spare[s % 2, 8] = jnp.where(inside, unit, rows)
        entry = {
            (i, j): jnp.broadcast_to(spare[s % 2, j, i : i + 1, :], (8, 128))
            for j in range(8)
            for i in range(j, 8)
        }
        y = [jnp.broadcast_to(spare[s % 2, 8, j : j + 1, :], (8, 128)) for j in range(8)]
        low = {}
        dinv = []
        for j in range(8):
            d = 1.0 / entry[j, j]
            dinv.append(d)
            for i in range(j + 1, 8):
                low[i, j] = entry[i, j] * d
            for i in range(j + 1, 8):
                for k in range(j + 1, i + 1):
                    entry[i, k] = entry[i, k] - low[i, j] * entry[k, j]
                y[i] = y[i] - low[i, j] * y[j]
        v = [None] * 8
        for j in reversed(range(8)):
            t = y[j] * dinv[j]
            for i in range(j + 1, 8):
                t = t - low[i, j] * v[i]
            v[j] = t
        order = [(s + 1 + g) % 16 for g in range(15)]
        for g in order:
            x = groups[g]
            t = jnp.where(inside, 0.0, x)
            for j in range(8):
                t = t - jnp.broadcast_to(x[:, lo+j:lo+j+1], (8, 128)) * v[j]
            groups[g] = t
        t = v[0]
        for j in range(1, 8):
            t = jnp.where(sub == j, v[j], t)
        groups[s] = t
    return groups


def mm(a, b, ca=1, cb=0):
    return lax.dot_general(a, b, (((ca,), (cb,)), ((), ())), precision=lax.Precision.HIGHEST, preferred_element_type=f32)

def solve_kernel(order_ref, rhs_ref, *refs):
    *piece_refs, out_ref, columns, gains, block, whole, spare = refs
    chans, n = rhs_ref.shape[1:]
    h = n // 2
    end = LAGS * n + chans
    count = 0
    for ref in piece_refs:
        for i in range(ref.shape[0]):
            start = pl.multiple_of(order_ref[count] * chans, chans)
            for k in range(LAGS):
                for j in range(LAGS - k):
                    columns[j, pl.ds((j + k) * n + start, chans), :] = ref[i, k]
            count += 1
    for j in range(LAGS):
        columns[j, LAGS * n :, :] = rhs_ref[j]
    row = lax.broadcasted_iota(jnp.int32, (n, n), 0)
    eye = row == lax.broadcasted_iota(jnp.int32, (n, n), 1)
    whiten = 0.1 * jnp.sum(jnp.where(eye, columns[0, :n], 0.0)) / n + 1e-06
    whiten = jnp.where(eye[:h, :h], whiten, 0.0)
    block[...] = columns[0, :h, :h] + whiten

    def first_half(p):
        inv = block[...]
        corner = columns[p, p * n + h : (p + 1) * n, :h]
        left = mm(corner, inv)
        whole[:h, :h] = inv
        whole[h:, :h] = left
        block[...] = columns[p, p * n + h : (p + 1) * n, h:] + whiten - mm(left, corner, 1, 1)

    def second_half(p):
        inv = block[...]
        left = whole[h:, :h]
        low = mm(inv, left)
        whole[:h, :h] += mm(left, low, 0, 0)
        whole[h:, :h] = -low
        whole[:h, h:] = -low.T
        whole[h:, h:] = inv
        below = (p + 1) * n
        gain = mm(columns[p, below:, :], whole[...])
        gains[p, below:, :] = gain
        for j in range(p + 1, LAGS):
            columns[j, j * n :, :] -= mm(gain[j * n - below :], columns[p, j * n : (j + 1) * n, :], 1, 1)
        if p + 1 < LAGS:
            block[...] = columns[p + 1, below : below + h, :h] + whiten

    def step(q, carry):
        even = 0.5 * (block[...] + block[...].T)
        groups = invert_128([even[8 * i : 8 * i + 8, :] for i in range(16)], spare)
        for i in range(16):
            block[8 * i : 8 * i + 8, :] = groups[i]
        for p in range(LAGS):
            pl.when(q == 2 * p)(lambda p=p: first_half(p))
            pl.when(q == 2 * p + 1)(lambda p=p: second_half(p))
        return carry

    lax.fori_loop(0, 2 * LAGS, step, 0)
    solved = {}
    for p in reversed(range(LAGS)):
        x = gains[p, LAGS * n : end, :]
        for j in range(p + 1, LAGS):
            x = x - mm(solved[j], gains[p, j * n : (j + 1) * n, :])
        solved[p] = x
        out_ref[p] = x.astype(out_ref.dtype)


def solve_filter(order, pieces, rhs):
    chans = rhs.shape[1]
    n = rhs.shape[2]
    half = n // 2
    return pl.pallas_call(
        solve_kernel,
        out_shape=jax.ShapeDtypeStruct((LAGS, chans, n), bf),
        in_specs=[pl.BlockSpec(memory_space=pltpu.SMEM)] + [VM] * (1 + len(pieces)),
        out_specs=VM,
        scratch_shapes=[
            pltpu.VMEM((LAGS, LAGS * n + chans, n), f32),
            pltpu.VMEM((LAGS, LAGS * n + chans, n), f32),
            pltpu.VMEM((half, half), f32),
            pltpu.VMEM((n, n), f32),
            pltpu.VMEM((2, 9, 8, half), f32),
        ],
        compiler_params=pltpu.CompilerParams(vmem_limit_bytes=40 * 2**20),
    )(order, rhs, *pieces)


def place(order_ref, piece_refs, shot, full):
    count = 0
    for ref in piece_refs:
        for i in range(ref.shape[0]):
            rows = ref.shape[2]
            full[pl.ds(pl.multiple_of(order_ref[count] * rows, rows), rows), :] = ref[i, shot]
            count += 1


def correlate_kernel(order_ref, own_ref, cos_ref, sin_ref, *refs):
    *piece_refs, out_ref, rotated, full = refs
    shots = piece_refs[0].shape[1]
    chans = piece_refs[0].shape[2]
    band = cos_ref.shape[1]
    for s in range(shots):
        place(order_ref, piece_refs, s, full)
        even = own_ref[s * chans : (s + 1) * chans, :band].astype(f32)
        odd = own_ref[s * chans : (s + 1) * chans, band:].astype(f32)
        for k in range(2 * LAGS):
            c, n = cos_ref[k : k + 1, :], sin_ref[k : k + 1, :]
            at = slice(k * chans, (k + 1) * chans)
            rotated[at, :band] = (even * c - odd * n).astype(bf)
            rotated[at, band:] = (odd * c + even * n).astype(bf)
        part = lax.dot_general(
            rotated[...], full[...], (((1,), (1,)), ((), ())), preferred_element_type=f32
        )
        if s == 0:
            out_ref[...] = part
        else:
            out_ref[...] += part


def correlate(order, own_rows, cosine, sine, pieces):
    width = own_rows.shape[1]
    chans = pieces[0].shape[2]
    channels = chans * order.shape[0]
    rows = 2 * LAGS * chans
    return pl.pallas_call(
        correlate_kernel,
        out_shape=jax.ShapeDtypeStruct((rows, channels), f32),
        in_specs=[pl.BlockSpec(memory_space=pltpu.SMEM)] + [VM] * (3 + len(pieces)),
        out_specs=VM,
        scratch_shapes=[pltpu.VMEM((rows, width), bf), pltpu.VMEM((channels, width), bf)],
        compiler_params=pltpu.CompilerParams(vmem_limit_bytes=40 * 2**20),
    )(order, own_rows, cosine, sine, *pieces)


def lag_moves():
    def move(dx, dy, dc):
        return [
            ((x * 4 + y) * 2 + c, ((x ^ dx) * 4 + (y + dy) % 4) * 2 + (c ^ dc))
            for x in range(2)
            for y in range(4)
            for c in range(2)
        ]

    return move(1, 0, 0), move(0, 1, 0), move(0, -1, 0), move(0, 0, 1)


def gather_lag(value):
    over_x, up, down, over_core = lag_moves()
    own = value[None]
    pair = jnp.concatenate([own, lax.ppermute(own, "lag", over_x)], axis=0)
    below = lax.ppermute(pair, "lag", up)
    above = lax.ppermute(pair, "lag", down)
    far_own = lax.ppermute(below[:1], "lag", up)
    far_other = lax.ppermute(above[1:], "lag", down)
    near = [pair, below, above, far_own, far_other]
    return near + [lax.ppermute(piece, "lag", over_core) for piece in near]


def lag_order():
    index = lax.axis_index("lag")
    x, y, core = index // 8, index // 2 % 4, index % 2
    places = [
        (x ^ dx) * 8 + (y + dy) % 4 * 2 + (core ^ dc)
        for dc in (0, 1)
        for dx, dy in ((0, 0), (1, 0), (0, 3), (1, 3), (0, 1), (1, 1), (0, 2), (1, 2))
    ]
    return jnp.stack(places).astype(jnp.int32)


def sum_over_shot(value):
    half = value.shape[0] // 2
    odd = lax.axis_index("shot") % 2 == 1

    def other(part, bit):
        return lax.ppermute(part, "shot", [(i, i ^ bit) for i in range(16)])

    first, second = value[:half], value[half:]
    held = jnp.where(odd, second, first) + other(jnp.where(odd, first, second), 1)
    for bit in (2, 4, 8):
        held = held + other(held, bit)
    back = other(held, 1)
    return jnp.where(odd, back, held), jnp.where(odd, held, back)


def shards(traces, live_mask, gap_samples):
    shot_count, local_chan, samples = traces.shape
    band_size = samples // 16
    live = live_mask.astype(f32)
    coarse = jnp.arange(samples // 2 // FINE, dtype=jnp.int32) * FINE
    waves = wave(coarse, samples, band_size) + wave(jnp.arange(FINE, dtype=jnp.int32), samples, band_size)
    own_rows = forward(traces, live, waves)
    own_spec = own_rows.reshape(shot_count, local_chan, 2 * band_size)
    order = lag_order()
    spectra = gather_lag(own_spec)
    spacing = samples // (2 * band_size)
    tap_delays = jnp.arange(LAGS, dtype=jnp.int32) * spacing
    lag_list = jnp.concatenate([tap_delays, gap_samples[0] + tap_delays])
    cosine, sine = wave(lag_list, samples, band_size)
    turn = jnp.where(jnp.arange(2 * LAGS) < LAGS, 1.0, -1.0).astype(f32)[:, None]
    partial_value = correlate(order, own_rows, cosine, turn * sine, spectra)
    channels = partial_value.shape[1]
    total_shots = shot_count * lax.axis_size("shot")
    scale = (1.0 / samples) * (1.0 / (samples * total_shots))
    shape = (LAGS, local_chan, channels)
    system, targets = sum_over_shot(partial_value)
    correlation = gather_lag((system * scale).reshape(shape))
    filter_bf = solve_filter(order, correlation, (targets * scale).reshape(shape))
    return inverse(order, filter_bf, spectra, own_rows, cosine[LAGS:], sine[LAGS:], live, waves, samples)


def solution(mesh):
    placed = (P("shot", "lag", None), P("shot", "lag"), P())
    return jax.shard_map(
        shards, mesh=mesh, in_specs=placed, out_specs=P("shot", "lag", None), check_vma=False
    )
```
